32 devices in a mesh: row: 4 (over y, core), col: 8 (over z, x).
Axes of the slice: x: 2, y: 2, z: 4, core: 2. Of those that a mesh axis runs over, the one named last changes fastest.
Arguments:
- modes: float32 [48, 2, 32, 1024], P(None, None, 'row', 'col'), may hold values from -25 to 25
- mean_flow: float32 [2, 32, 1024], P(None, 'row', 'col'), may hold values from -5 to 5
- seeds: int32 [4096, 48], P(('row', 'col')), may hold values from 0 to 4095
- amplitudes: float32 [48], replicated, may hold values from 0.5 to 2
- water_mask: int32 [32, 1024], P('row', 'col'), may hold values 0 or 1
Outputs:
- new_modes: float32 [48, 2, 32, 1024], P(None, None, 'row', 'col')
- new_coeffs: float32 [4096, 48], P(('row', 'col'))
The draws below stay inside these ranges and needn't reach their ends.
Inputs may be any that keep to these rules, and one draw needn't show every extreme that they name: `water_mask`: 1 marks a water cell, 0 a land cell.
All inputs are finite; a program needn't handle non-finite values. No bound on the sum of `water_mask` on one device may be relied on, other than what follows from the above.
Results may differ from the reference program's by a relative error of at most 0.0003.
Values sent between devices are 32-bit elements; how exact they have to be, the bound alone decides.
No kernel may reach another device: no remote copies, remote signals or barrier semaphores. Data moves between devices by JAX's collectives and lax.ppermute only.
A program may use at most 128 MiB of HBM per device.

```python
import math
import jax
import jax.numpy as jnp
from jax import lax

S = 48
NX = 32
NY = 1024
R = 4096


def lattice_field(key, count):
    subkeys = jax.random.split(key, 5)
    x_cells = jnp.arange(NX, dtype=jnp.float32)[:, None]
    y_cells = jnp.arange(NY, dtype=jnp.float32)[None, :]
    wave_x = jax.random.randint(subkeys[0], (count, 2, 3), -2, 3).astype(jnp.float32)
    wave_y = jax.random.randint(subkeys[1], (count, 2, 3), -2, 3).astype(jnp.float32)
    phases = jax.random.uniform(subkeys[2], (count, 2, 3), jnp.float32, -math.pi, math.pi)
    wave_amp = jax.random.uniform(subkeys[3], (count, 2, 3), jnp.float32, -1.0, 1.0)
    smooth = jnp.zeros((count, 2, NX, NY), jnp.float32)
    for number in range(3):
        argument = 2.0 * math.pi / 32.0 * (wave_x[:, :, number, None, None] * x_cells + wave_y[:, :, number, None, None] * y_cells) + phases[:, :, number, None, None]
        smooth = smooth + wave_amp[:, :, number, None, None] * jnp.cos(argument)
    rough_part = jnp.clip(jax.random.normal(subkeys[4], (count, 2, NX, NY), jnp.float32), -4.0, 4.0)
    return smooth + 0.5 * rough_part


def draw_modes(key, part):
    own_part = lattice_field(jax.random.fold_in(key, 11), S)
    shared = lattice_field(jax.random.fold_in(key, 12), 1)
    loadings = jax.random.uniform(jax.random.fold_in(key, 13), (S, 1, 1, 1), jnp.float32, 0.5, 1.5)
    field = own_part + loadings * shared
    return field


def draw_mean_flow(key, part):
    return lattice_field(jax.random.fold_in(key, 21), 1)[0]


def set_ends(entries, key, least, top_value):
    index_at = [jax.random.randint(jax.random.fold_in(key, axis), (), 0, length) for axis, length in enumerate(entries.shape)]
    longest = entries.shape.index(max(entries.shape))
    next_to = index_at[:longest] + [(index_at[longest] + 1) % entries.shape[longest]] + index_at[longest + 1:]
    return entries.at[tuple(index_at)].set(least).at[tuple(next_to)].set(top_value)


def setup_inputs(seed: int = 0) -> dict:
    streams_of = jax.random.split(jax.random.key(seed), 6)
    return {
        "modes": draw_modes(jax.random.fold_in(streams_of[5], 71), 0),
        "mean_flow": draw_mean_flow(jax.random.fold_in(streams_of[5], 71), 0),
        "seeds": set_ends(jax.random.randint(streams_of[2], (R, S), 0, 4096), jax.random.fold_in(streams_of[2], 1), 0, 4095).astype(jnp.int32),
        "amplitudes": jnp.clip(jnp.exp(jax.random.uniform(streams_of[3], (S,), jnp.float32, math.log(0.5), math.log(2.0))), 0.5, 2.0),
        "water_mask": set_ends((jax.random.randint(streams_of[4], (NX, NY), 0, 8) < 7).astype(jnp.int32), jax.random.fold_in(streams_of[4], 1), 0, 1),
    }


TIME_STEP = 0.25
VISCOUS = 0.2
PRECISE = lax.Precision.HIGHEST

def matmul(left_side, right_side):
    return jnp.dot(left_side.astype(jnp.float32), right_side.astype(jnp.float32), precision=PRECISE, preferred_element_type=jnp.float32)

def matmul_nt(left_side, right_side):
    return lax.dot_general(left_side.astype(jnp.float32), right_side.astype(jnp.float32), (((1,), (1,)), ((), ())), precision=PRECISE, preferred_element_type=jnp.float32)

def factor_solve(factor, right_side):
    lower_part = lax.linalg.triangular_solve(factor, right_side, left_side=True, lower=True)
    return lax.linalg.triangular_solve(factor, lower_part, left_side=True, lower=True, transpose_a=True)

def raw_coeffs(seeds, amplitudes, first_row, row_total):
    phases = seeds.astype(jnp.float32) * (3.0 * math.pi / 8192.0)
    row_ids = (first_row + jnp.arange(seeds.shape[0], dtype=jnp.int32)).astype(jnp.float32)
    strength = 0.5 + row_ids / row_total
    return strength[:, None] * amplitudes[None, :] * (jnp.cos(phases) + 0.5 * jnp.cos(2.0 * phases))

def pair_products(coeffs):
    return (coeffs[:, :, None] * coeffs[:, None, :]).reshape(coeffs.shape[0], -1)

def derivatives(padded):
    along_x = 0.5 * (padded[:, :, 2:, 1:-1] - padded[:, :, :-2, 1:-1])
    along_y = 0.5 * (padded[:, :, 1:-1, 2:] - padded[:, :, 1:-1, :-2])
    return (along_x, along_y)

def transport_term(advecting_velocity, gradient_east, gradient_north):
    return advecting_velocity[..., 0:1, :, :] * gradient_east + advecting_velocity[..., 1:2, :, :] * gradient_north

def reference(modes, mean_flow, seeds, amplitudes, water_mask):
    mode_count = modes.shape[0]
    uncentered = raw_coeffs(seeds, amplitudes, 0, R)
    coeffs = uncentered - jnp.sum(uncentered, axis=0) / R
    pair_terms = pair_products(coeffs)
    covariance = matmul(coeffs.T, coeffs) / R
    third_moment = matmul(coeffs.T, pair_terms) / R
    weight_map = factor_solve(jnp.linalg.cholesky(covariance), third_moment)
    weight_cube = weight_map.reshape(mode_count, mode_count, mode_count)
    stacked_fields = jnp.concatenate([modes, mean_flow[None]], axis=0)
    padded = jnp.pad(stacked_fields, ((0, 0), (0, 0), (1, 1), (1, 1)))
    grad_x, grad_y = derivatives(padded)
    water_cells = water_mask.astype(jnp.float32)
    weight_scale = 1.0 / (2.0 * NX * NY)
    mode_grad_x = grad_x[:mode_count]
    mode_grad_y = grad_y[:mode_count]
    linear = -(transport_term(mean_flow, mode_grad_x, mode_grad_y) + transport_term(modes, grad_x[mode_count:], grad_y[mode_count:]))
    flat_modes = modes.reshape(mode_count, -1)
    weighted = (modes * (water_cells * weight_scale)).reshape(mode_count, -1)
    gram_matrix = matmul_nt(weighted, flat_modes)
    linear_projection = matmul_nt(weighted, linear.reshape(mode_count, -1))

    def advance(nonlinear, position):
        single = lax.dynamic_index_in_dim(modes, position, 0, keepdims=False)
        pair_field = (single[0:1] * mode_grad_x + single[1:2] * mode_grad_y).reshape(mode_count, -1)
        column = -matmul_nt(weighted, pair_field)
        weight_slice = lax.dynamic_index_in_dim(weight_cube, position, 1, keepdims=False)
        return (nonlinear + matmul(weight_slice, pair_field), column)
    nonlinear, columns = lax.scan(advance, jnp.zeros_like(flat_modes), jnp.arange(mode_count, dtype=jnp.int32))
    tensor = jnp.transpose(columns, (1, 0, 2)).reshape(mode_count, -1)
    forcing = water_cells * (linear - nonlinear.reshape(modes.shape))
    projected = matmul_nt(weighted, forcing.reshape(mode_count, -1))
    factor = jnp.linalg.cholesky(gram_matrix)
    solved = factor_solve(factor, projected)
    correction = matmul(solved.T, flat_modes).reshape(modes.shape)
    half_step = water_cells * (modes + TIME_STEP * (forcing - correction))
    beside_all = jnp.pad(half_step, ((0, 0), (0, 0), (1, 1), (1, 1)))
    laplace_term = beside_all[:, :, 2:, 1:-1] + beside_all[:, :, :-2, 1:-1] + beside_all[:, :, 1:-1, 2:] + beside_all[:, :, 1:-1, :-2] - 4.0 * half_step
    new_modes = water_cells * (half_step + VISCOUS * laplace_term)
    drift = matmul(coeffs, linear_projection.T) + matmul(pair_terms - covariance.reshape(1, -1), tensor.T)
    change = factor_solve(factor, drift.T).T
    new_coeffs = coeffs + TIME_STEP * change
    return (new_modes, new_coeffs)
```

```python
import functools
import math

import jax
import jax.numpy as jnp
import numpy as np
from jax import lax
from jax.experimental import pallas as pl
from jax.experimental.pallas import tpu as pltpu
from jax.sharding import PartitionSpec as P

TIME_STEP = 0.25
VISCOUS = 0.2
PRECISE = lax.Precision.HIGHEST
TILE = 8
LANES = 128
NT = (((1,), (1,)), ((), ()))
NN = (((1,), (0,)), ((), ()))


def pair_start(block):
    return TILE * TILE * block * (block + 1) // 2


def pair_layout(count):
    blocks = count // TILE
    pairs = pair_start(blocks)
    padded = -(-(pairs + count + 1) // LANES) * LANES
    first = np.full((1, padded), -1, np.int32)
    second = np.full((1, padded), -1, np.int32)
    share = np.zeros((1, padded), np.float32)
    for block in range(blocks):
        for j in range(TILE * (block + 1)):
            start = pair_start(block) + TILE * j
            first[0, start : start + TILE] = j
            second[0, start : start + TILE] = TILE * block + np.arange(TILE)
            share[0, start : start + TILE] = 0.5 if j // TILE == block else 1.0
    share[0, pairs : pairs + count] = 1.0
    return pairs, padded, first, second, share


def dot32(left, right, dims):
    return lax.dot_general(left, right, dims, precision=PRECISE, preferred_element_type=jnp.float32)


def halves(values):
    high = values.astype(jnp.bfloat16)
    low = (values - high.astype(jnp.float32)).astype(jnp.bfloat16)
    return high, low


def stacked_halves(values):
    high, low = halves(values)
    return jnp.concatenate([high, low], axis=0)


def dot_halves(left_stack, right, dims):
    high, low = halves(right)
    both = lax.dot_general(left_stack, high, dims, preferred_element_type=jnp.float32)
    both += lax.dot_general(left_stack, low, dims, preferred_element_type=jnp.float32)
    rows = left_stack.shape[0] // 2
    return both[:rows] + both[rows:]


def lane_ids(rows):
    return lax.broadcasted_iota(jnp.int32, (rows, LANES), 1)


def pack_kernel(modes, mean_flow, water, planes, col_first, col_last):
    count = planes.shape[0] // 2
    step = modes.shape[0] // (2 * count)
    fields = planes.shape[1]
    ids = lane_ids(fields)
    first = jnp.zeros((fields, LANES), jnp.float32)
    last = jnp.zeros((fields, LANES), jnp.float32)
    planes[:, step:, :] = jnp.zeros((2 * count, fields - step, LANES), jnp.float32)
    for x in range(count):
        for c in range(2):
            q = 2 * x + c
            planes[q, 0:step, :] = modes[pl.ds(c * count + x, step, stride=2 * count), :]
            planes[q, step : step + 1, :] = mean_flow[c * count + x : c * count + x + 1, :]
            planes[q, step + 1 : step + 2, :] = water[x : x + 1, :].astype(jnp.float32)
            plane = planes[q]
            first = jnp.where(ids == q, pltpu.roll(plane, q, 1), first)
            last = jnp.where(ids == q, pltpu.roll(plane, q + 1, 1), last)
    col_first[...] = first
    col_last[...] = last


def moment_kernel(scale, coeffs, planes, sums, rows):
    count = coeffs.shape[0]
    pairs = pair_start(count // TILE)
    values = coeffs[...]
    fill_coeff_rows(values, rows)
    rows[pairs + count : pairs + count + 1, :] = jnp.ones((1, values.shape[1]), jnp.float32)
    padded = rows.shape[0]
    sums[:, :padded] = dot32(values, rows[...], NT)
    gram = jnp.zeros((count, count), jnp.float32)
    for x in range(planes.shape[0] // 2):
        water = planes[2 * x, count + 1 : count + 2, :] * scale
        for c in range(2):
            field = planes[2 * x + c, 0:count, :]
            gram += dot32(field * water, field, NT)
    sums[:, padded:] = jnp.zeros((count, sums.shape[1] - padded), jnp.float32)
    sums[:, padded : padded + count] = gram


def fill_coeff_rows(values, rows):
    count = values.shape[0]
    blocks = count // TILE
    pairs = pair_start(blocks)
    for j in range(count):
        row = values[j : j + 1, :]
        for block in range(j // TILE, blocks):
            start = pair_start(block) + TILE * j
            rows[start : start + TILE, :] = row * values[TILE * block : TILE * block + TILE, :]
    rows[pairs : pairs + count, :] = values
    rows[pairs + count :, :] = jnp.zeros((rows.shape[0] - pairs - count, values.shape[1]), jnp.float32)


def gradient_kernel(planes, above, below, left, right, grad_x, grad_y):
    total = planes.shape[0]
    fields = planes.shape[1]
    ids = lane_ids(fields)
    from_left = left[...]
    from_right = right[...]
    for q in range(total):
        before = above[q] if q < 2 else planes[q - 2]
        after = below[q - total + 2] if q >= total - 2 else planes[q + 2]
        grad_x[q] = 0.5 * (after - before)
        plane = planes[q]
        east = jnp.where(ids == LANES - 1, pltpu.roll(from_right, LANES - 1 - q, 1), pltpu.roll(plane, LANES - 1, 1))
        west = jnp.where(ids == 0, pltpu.roll(from_left, (LANES - q) % LANES, 1), pltpu.roll(plane, 1, 1))
        grad_y[q] = 0.5 * (east - west)


def fill_pair_fields(x, planes, grad_x, grad_y, rows):
    count = planes.shape[1] // TILE * TILE - TILE
    blocks = count // TILE
    pairs = pair_start(blocks)
    q = 2 * x
    refs = [planes.at[q], planes.at[q + 1]]
    grads = [(grad_x.at[q], grad_y.at[q]), (grad_x.at[q + 1], grad_y.at[q + 1])]
    for j in range(count + 1):
        one = slice(j, j + 1)
        u_j = [ref[one, :] for ref in refs]
        g_j = [(gx[one, :], gy[one, :]) for gx, gy in grads]
        for block in range(j // TILE if j < count else 0, blocks):
            start = pair_start(block) + TILE * j if j < count else pairs + TILE * block
            tile = slice(TILE * block, TILE * block + TILE)
            u_k = [ref[tile, :] for ref in refs]
            for c in range(2):
                gx, gy = grads[c]
                value = u_j[0] * gx[tile, :] + u_j[1] * gy[tile, :] + u_k[0] * g_j[c][0] + u_k[1] * g_j[c][1]
                rows[start : start + TILE, c * LANES : (c + 1) * LANES] = value


def tensor_kernel(scale, planes, grad_x, grad_y, out, rows, total):
    count = out.shape[0]
    used = pair_start(count // TILE) + count
    rows[used:, :] = jnp.zeros((rows.shape[0] - used, rows.shape[1]), jnp.float32)
    total[...] = jnp.zeros_like(total)

    def body(x, carry):
        fill_pair_fields(x, planes, grad_x, grad_y, rows)
        water = planes[2 * x, count + 1 : count + 2, :] * (-scale)
        weighted = jnp.concatenate([planes[2 * x, 0:count, :] * water, planes[2 * x + 1, 0:count, :] * water], axis=1)
        stack = stacked_halves(weighted)
        for start in range(0, rows.shape[0], 256):
            stop = min(start + 256, rows.shape[0])
            total[:, start:stop] += dot_halves(stack, rows[start:stop, :], NT)
        return carry

    lax.fori_loop(0, planes.shape[0] // 2, body, 0)
    out[...] = total[...]


def inverse_pair(first, second):
    count = first.shape[0]
    row_ids = lax.broadcasted_iota(jnp.int32, (count, count), 0)
    col_ids = lax.broadcasted_iota(jnp.int32, (count, count), 1)
    both = [first, second]
    for k in range(count):
        for n in range(2):
            a = both[n]
            row = a[k : k + 1, :]
            col = a[:, k : k + 1]
            pivot = 1.0 / a[k : k + 1, k : k + 1]
            row = jnp.where(col_ids[0:1] == k, 1.0, row) * pivot
            kept = jnp.where(col_ids == k, 0.0, a)
            both[n] = jnp.where(row_ids == k, row, kept - col * row)
    return both


def solve_kernel(realizations, sums, first, second, share, weights, gram_inverse, mean, pair_cov):
    count = weights.shape[0]
    padded = weights.shape[1]
    pairs = pair_start(count // TILE)
    everything = sums[...]
    raw_second = everything[:, pairs : pairs + count] * (1.0 / realizations)
    means = everything[:, pairs + count : pairs + count + 1] * (1.0 / realizations)
    gram = everything[:, padded : padded + count]
    row_ids = lax.broadcasted_iota(jnp.int32, (count, count), 0)
    col_ids = lax.broadcasted_iota(jnp.int32, (count, count), 1)
    mean_row = jnp.sum(jnp.where(row_ids == col_ids, means, 0.0), axis=0, keepdims=True)
    covariance = raw_second - means * mean_row
    cov_inverse, gram_inv = inverse_pair(covariance, gram)
    ids = lax.broadcasted_iota(jnp.int32, (count, padded), 0)
    pick_first = (ids == first[...]).astype(jnp.float32)
    pick_second = (ids == second[...]).astype(jnp.float32)
    cov_first = dot32(covariance, pick_first, NN)
    cov_second = dot32(covariance, pick_second, NN)
    mean_first = jnp.sum(pick_first * means, axis=0, keepdims=True)
    mean_second = jnp.sum(pick_second * means, axis=0, keepdims=True)
    cov_pair = jnp.sum(pick_first * cov_second, axis=0, keepdims=True)
    third = everything[:, :padded] * (1.0 / realizations) - (
        means * (cov_pair + mean_first * mean_second) + mean_first * cov_second + mean_second * cov_first
    )
    shares = share[...]
    weight_map = dot32(cov_inverse, third, NN) * shares
    lanes = lax.broadcasted_iota(jnp.int32, (count, padded), 1)
    unit = jnp.where(lanes - pairs == ids, 1.0, 0.0)
    weights[...] = jnp.where(lanes < pairs, weight_map, unit)
    gram_inverse[...] = gram_inv
    mean[...] = jnp.broadcast_to(means, mean.shape)
    pair_cov[...] = cov_pair * shares


def forcing_kernel(start_plane, weights, planes, grad_x, grad_y, out, rows):
    count = weights.shape[0]
    used = pair_start(count // TILE) + count
    rows[used:, :] = jnp.zeros((rows.shape[0] - used, rows.shape[1]), jnp.float32)
    stack = stacked_halves(weights[...])

    def body(n, carry):
        x = start_plane + n
        fill_pair_fields(x, planes, grad_x, grad_y, rows)
        nonlinear = dot_halves(stack, rows[...], NN)
        water = planes[2 * x, count + 1 : count + 2, :]
        for c in range(2):
            part = nonlinear[:, c * LANES : (c + 1) * LANES]
            out[2 * n + c] = water * (planes[2 * x + c, 0:count, :] - TIME_STEP * part)
        return carry

    lax.fori_loop(0, out.shape[0] // 2, body, 0)


def edge_kernel(moved, col_first, col_last):
    total, count, _ = moved.shape
    ids = lane_ids(count)
    first = jnp.zeros((count, LANES), jnp.float32)
    last = jnp.zeros((count, LANES), jnp.float32)
    for q in range(total):
        plane = moved[q]
        first = jnp.where(ids == q, pltpu.roll(plane, q, 1), first)
        last = jnp.where(ids == q, pltpu.roll(plane, q + 1, 1), last)
    col_first[...] = first
    col_last[...] = last


def finish_kernel(
    tensor, weights, gram_inverse, coeffs, mean, pair_cov, share,
    planes, above, below, left, right,
    moved, moved_above, moved_below, moved_left, moved_right,
    new_modes, new_coeffs, half, rows,
):
    count = weights.shape[0]
    total = planes.shape[0]
    inverse = gram_inverse[...]
    tens = tensor[...]
    solved = dot32(dot32(weights[...], tens, NT), inverse, NN) * TIME_STEP
    ids = lane_ids(count)

    def corrected(value, field, water):
        return value - water * dot32(solved, field, NN)

    for q in range(2):
        water = above[0, count + 1 : count + 2, :]
        half[q] = corrected(moved_above[q], above[q, 0:count, :], water)
        water = below[0, count + 1 : count + 2, :]
        half[total + 2 + q] = corrected(moved_below[q], below[q, 0:count, :], water)
    for q in range(total):
        water = planes[q, count + 1 : count + 2, :]
        half[q + 2] = corrected(moved[q], planes[q, 0:count, :], water)
    half_left = corrected(moved_left[...], left[0:count, :], left[count + 1 : count + 2, :])
    half_right = corrected(moved_right[...], right[0:count, :], right[count + 1 : count + 2, :])
    for q in range(total):
        plane = half[q + 2]
        east = jnp.where(ids == LANES - 1, pltpu.roll(half_right, LANES - 1 - q, 1), pltpu.roll(plane, LANES - 1, 1))
        west = jnp.where(ids == 0, pltpu.roll(half_left, (LANES - q) % LANES, 1), pltpu.roll(plane, 1, 1))
        laplace = half[q] + half[q + 4] + east + west - 4.0 * plane
        water = planes[q, count + 1 : count + 2, :]
        x, c = q // 2, q % 2
        new_modes[pl.ds(c * (total // 2) + x, count, stride=total), :] = water * (plane + VISCOUS * laplace)

    centered = coeffs[...] - mean[...]
    fill_coeff_rows(centered, rows)
    drift = dot32(tens * share[...], rows[...], NN)
    drift -= jnp.sum(tens * pair_cov[...], axis=1, keepdims=True)
    new_coeffs[...] = (centered + TIME_STEP * dot32(inverse, drift, NN)).T


def swap_bit(values, axis, bit):
    count = lax.axis_size(axis)
    return lax.ppermute(values, axis, [(i, i ^ bit) for i in range(count)])


def axis_bits(axis):
    count = lax.axis_size(axis)
    bits = []
    while (1 << len(bits)) < count:
        bits.append(1 << len(bits))
    return [(axis, bit) for bit in bits]


def total_over_mesh(values):
    for axis in ("row", "col"):
        if lax.axis_size(axis) & (lax.axis_size(axis) - 1):
            return lax.psum(values, ("row", "col"))
    steps = axis_bits("row") + axis_bits("col")
    if not steps:
        return values
    rows = values.shape[0] // 2
    near_axis, near_bit = steps[0]
    lower = lax.axis_index(near_axis) % 2 == 0
    top, bottom = values[:rows], values[rows:]
    kept = jnp.where(lower, top, bottom) + swap_bit(jnp.where(lower, bottom, top), near_axis, near_bit)
    for axis, bit in steps[1:]:
        kept = kept + swap_bit(kept, axis, bit)
    other = swap_bit(kept, near_axis, near_bit)
    return jnp.concatenate([jnp.where(lower, kept, other), jnp.where(lower, other, kept)], axis=0)


def from_before(values, axis):
    count = lax.axis_size(axis)
    return lax.ppermute(values, axis, [(i, i + 1) for i in range(count - 1)])


def from_after(values, axis):
    count = lax.axis_size(axis)
    return lax.ppermute(values, axis, [(i + 1, i) for i in range(count - 1)])


def raw_coeffs(seeds, amplitudes, first_row, row_total):
    phases = seeds.astype(jnp.float32) * (3.0 * math.pi / 8192.0)
    row_ids = (first_row + jnp.arange(seeds.shape[0], dtype=jnp.int32)).astype(jnp.float32)
    strength = 0.5 + row_ids / row_total
    return strength[:, None] * amplitudes[None, :] * (jnp.cos(phases) + 0.5 * jnp.cos(2.0 * phases))


def shape32(*dims):
    return jax.ShapeDtypeStruct(dims, jnp.float32)


def vmem32(*dims):
    return pltpu.VMEM(dims, jnp.float32)


PARAMS = pltpu.CompilerParams(vmem_limit_bytes=32 * 1024 * 1024)


def on_device(modes, mean_flow, seeds, amplitudes, water_mask):
    count, _, nx, ny = modes.shape
    devices = lax.axis_size("row") * lax.axis_size("col")
    rows_dev = seeds.shape[0]
    row_total = rows_dev * devices
    scale = 1.0 / (2.0 * nx * ny * devices)
    pairs, padded, first, second, share = pair_layout(count)
    wide = padded + LANES
    fields = count + TILE
    call = functools.partial(pl.pallas_call, compiler_params=PARAMS)

    planes, col_first, col_last = call(
        pack_kernel,
        out_shape=(shape32(2 * nx, fields, ny), shape32(fields, ny), shape32(fields, ny)),
    )(modes.reshape(count * 2 * nx, ny), mean_flow.reshape(2 * nx, ny), water_mask)
    above = from_before(planes[2 * nx - 2 :], "row")
    below = from_after(planes[:2], "row")
    left = from_before(col_last, "col")
    right = from_after(col_first, "col")

    first_row = lax.axis_index(("row", "col")) * rows_dev
    coeffs = raw_coeffs(seeds, amplitudes, first_row, row_total).T
    sums = call(
        functools.partial(moment_kernel, scale),
        out_shape=shape32(count, wide),
        scratch_shapes=[vmem32(padded, rows_dev)],
    )(coeffs, planes)
    sums = total_over_mesh(sums)

    grad_x, grad_y = call(
        gradient_kernel, out_shape=(shape32(2 * nx, fields, ny), shape32(2 * nx, fields, ny))
    )(planes, above, below, left, right)
    tensor = call(
        functools.partial(tensor_kernel, scale),
        out_shape=shape32(count, padded),
        scratch_shapes=[vmem32(padded, 2 * ny), vmem32(count, padded)],
    )(planes, grad_x, grad_y)
    tensor = total_over_mesh(tensor)

    weights, gram_inverse, mean, pair_cov = call(
        functools.partial(solve_kernel, row_total),
        out_shape=(shape32(count, padded), shape32(count, count), shape32(count, rows_dev), shape32(1, padded)),
    )(sums, first, second, share)

    pieces = []
    for start in range(0, nx, nx // 4):
        pieces.append(
            call(
                functools.partial(forcing_kernel, start),
                out_shape=shape32(2 * (nx // 4), count, ny),
                scratch_shapes=[vmem32(padded, 2 * ny)],
            )(weights, planes, grad_x, grad_y)
        )
    moved = jnp.concatenate(pieces, axis=0)
    moved_first, moved_last = call(edge_kernel, out_shape=(shape32(count, ny), shape32(count, ny)))(moved)
    moved_above = from_before(moved[2 * nx - 2 :], "row")
    moved_below = from_after(moved[:2], "row")
    moved_left = from_before(moved_last, "col")
    moved_right = from_after(moved_first, "col")

    new_modes, new_coeffs = call(
        finish_kernel,
        out_shape=(shape32(count * 2 * nx, ny), shape32(rows_dev, count)),
        scratch_shapes=[vmem32(2 * nx + 4, count, ny), vmem32(padded, rows_dev)],
    )(
        tensor, weights, gram_inverse, coeffs, mean, pair_cov, share,
        planes, above, below, left, right,
        moved, moved_above, moved_below, moved_left, moved_right,
    )
    return (new_modes.reshape(modes.shape), new_coeffs)


def solution(mesh):
    return jax.shard_map(
        on_device,
        mesh=mesh,
        in_specs=(
            P(None, None, "row", "col"),
            P(None, "row", "col"),
            P(("row", "col"), None),
            P(),
            P("row", "col"),
        ),
        out_specs=(P(None, None, "row", "col"), P(("row", "col"), None)),
        check_vma=False,
    )
```

```python
import functools
import math

import jax
import jax.numpy as jnp
import numpy as np
from jax import lax
from jax.experimental import pallas as pl
from jax.experimental.pallas import tpu as pltpu
from jax.sharding import PartitionSpec as P

TIME_STEP = 0.25
VISCOUS = 0.2
PRECISE = lax.Precision.HIGHEST
TILE = 8
LANES = 128
NT = (((1,), (1,)), ((), ()))
NN = (((1,), (0,)), ((), ()))


HALF_TILE = TILE // 2


def pair_start(block):
    return TILE * (TILE * block * (block - 1) // 2 + (HALF_TILE + 1) * block)


def pair_layout(count):
    blocks = count // TILE
    pairs = pair_start(blocks)
    padded = -(-(pairs + count + 2) // LANES) * LANES
    first = np.full((1, padded), -1, np.int32)
    second = np.full((1, padded), -1, np.int32)
    share = np.zeros((1, padded), np.float32)

    def put(row, j, k):
        first[0, row], second[0, row], share[0, row] = j, k, 0.5 if j == k else 1.0

    for block in range(blocks):
        row = pair_start(block)
        base = TILE * block
        for j in range(base):
            for r in range(TILE):
                put(row + TILE * j + r, j, base + r)
        row += TILE * base
        for n in range(HALF_TILE + 1):
            for r in range(TILE):
                if r >= n:
                    put(row + TILE * n + r, base + n, base + r)
                elif n < HALF_TILE:
                    put(row + TILE * n + r, base + TILE - n, base + TILE - n + r)
    share[0, pairs : pairs + count] = 1.0
    return pairs, padded, first, second, share


def pair_tiles(arrays, count):
    blocks = count // TILE
    ids = lax.broadcasted_iota(jnp.int32, (TILE, arrays[0].shape[1]), 0)

    def tile(block):
        return [a[TILE * block : TILE * block + TILE, :] for a in arrays]

    for j in range(count):
        leads = [a[j : j + 1, :] for a in arrays]
        for block in range(j // TILE + 1, blocks):
            yield pair_start(block) + TILE * j, leads, tile(block)
    for block in range(blocks):
        base = TILE * block
        for n in range(HALF_TILE + 1):
            leads, parts = [a[base + n : base + n + 1, :] for a in arrays], tile(block)
            if 0 < n < HALF_TILE:
                other = base + TILE - n
                leads = [jnp.where(ids < n, a[other : other + 1, :], lead) for a, lead in zip(arrays, leads)]
                parts = [jnp.where(ids < n, pltpu.roll(part, n, 0), part) for part in parts]
            yield pair_start(block) + TILE * (base + n), leads, parts


def flow_tiles(arrays, count):
    leads = [a[count : count + 1, :] for a in arrays]
    for block in range(count // TILE):
        rows = slice(TILE * block, TILE * block + TILE)
        yield pair_start(count // TILE) + TILE * block, leads, [a[rows, :] for a in arrays]


def dot32(left, right, dims):
    return lax.dot_general(left, right, dims, precision=PRECISE, preferred_element_type=jnp.float32)


def halves(values):
    high = values.astype(jnp.bfloat16)
    low = (values - high.astype(jnp.float32)).astype(jnp.bfloat16)
    return high, low


def stacked_halves(values):
    high, low = halves(values)
    return jnp.concatenate([high, low], axis=0)


def dot_halves(left_stack, right, dims):
    high, low = halves(right)
    both = lax.dot_general(left_stack, high, dims, preferred_element_type=jnp.float32)
    both += lax.dot_general(left_stack, low, dims, preferred_element_type=jnp.float32)
    rows = left_stack.shape[0] // 2
    return both[:rows] + both[rows:]


def lane_ids(rows):
    return lax.broadcasted_iota(jnp.int32, (rows, LANES), 1)


SECOND = 32
SIDE = 64


def put_lane(packed, ids, plane, lane, target):
    return jnp.where(ids == target, pltpu.roll(plane, (target - lane) % LANES, 1), packed)


def front_kernel(
    scale, modes, flow, water, seeds, strength, amplitudes, planes, col_first, col_last, sums, early, coeffs, rows
):
    step = coeffs.shape[0]
    total = modes.shape[0] // step
    nx = total // 2
    fields = planes.shape[1]
    planes[...] = jnp.zeros(planes.shape, jnp.float32)
    diagonal = lax.broadcasted_iota(jnp.int32, (step, step), 0) == lax.broadcasted_iota(jnp.int32, (step, step), 1)
    heights = jnp.sum(jnp.where(diagonal, amplitudes[...], 0.0), axis=1, keepdims=True)
    wave = jnp.cos(seeds[...].astype(jnp.float32) * (3.0 * math.pi / 8192.0))
    values = strength[...] * heights * (wave + (wave * wave - 0.5))
    coeffs[...] = values
    pairs = pair_start(step // TILE)
    fill_coeff_rows(values, rows)
    rows[pairs + step : pairs + step + 1, :] = jnp.ones((1, values.shape[1]), jnp.float32)
    moments = dot32(values, rows[...], NT)
    tiles = moments.shape[1] // LANES
    for tile in range(tiles):
        sums[tile * step : (tile + 1) * step, :] = moments[:, tile * LANES : (tile + 1) * LANES]
    ids = lane_ids(fields)
    first = jnp.zeros((fields, LANES), jnp.float32)
    last = jnp.zeros((fields, LANES), jnp.float32)
    gram = jnp.zeros((step, step), jnp.float32)
    for x in range(nx):
        mask = water[x : x + 1, :].astype(jnp.float32)
        both = []
        for c in range(2):
            q = 2 * x + c
            field = modes[pl.ds(c * nx + x, step, stride=total), :]
            both.append(field)
            planes[q + 4, 0:step, :] = field
            planes[q + 4, step : step + 1, :] = flow[c * nx + x : c * nx + x + 1, :]
            planes[q + 4, step + 1 : step + 2, :] = mask
            plane = planes[q + 4]
            first = put_lane(first, ids, plane, 0, q + 2)
            first = put_lane(first, ids, plane, 1, q + 2 + SECOND)
            last = put_lane(last, ids, plane, LANES - 1, q + 2)
            last = put_lane(last, ids, plane, LANES - 2, q + 2 + SECOND)
        wide = jnp.concatenate(both, axis=1)
        weight = jnp.concatenate([mask, mask], axis=1) * scale
        gram += dot_halves(stacked_halves(wide * weight), wide, NT)
    col_first[...] = first
    col_last[...] = last
    heads = lax.broadcasted_iota(jnp.int32, (step, step), 0)
    lanes = lax.broadcasted_iota(jnp.int32, (step, step), 1)
    both = jnp.where(lanes < heads, gram, moments[:, pairs : pairs + step])
    corner = jnp.sum(jnp.where(lanes == heads, gram, 0.0), axis=1, keepdims=True)
    rest = jnp.zeros((step, SIDE - step - 2), jnp.float32)
    packed = jnp.concatenate([both, moments[:, pairs + step : pairs + step + 1], corner, rest], axis=1)
    early[...] = jnp.concatenate([packed[: step // 2], packed[step // 2 :]], axis=1)


def fill_coeff_rows(values, rows):
    count = values.shape[0]
    pairs = pair_start(count // TILE)
    for start, (lead,), (part,) in pair_tiles([values], count):
        rows[start : start + TILE, :] = lead * part
    rows[pairs : pairs + count, :] = values
    rows[pairs + count :, :] = jnp.zeros((rows.shape[0] - pairs - count, values.shape[1]), jnp.float32)


def extend_kernel(planes, above, below, first_in, last_in, extended, col_first, col_last):
    total = planes.shape[0]
    fields = planes.shape[1]
    ids = lane_ids(fields)
    extended[0:4] = above[...]
    extended[4 : total - 4] = planes[4 : total - 4]
    extended[total - 4 :] = below[...]
    first = first_in[...]
    last = last_in[...]
    for c in range(2):
        for plane, lane in ((above[2 + c], c), (below[c], total - 6 + c)):
            first = put_lane(first, ids, plane, 0, lane)
            last = put_lane(last, ids, plane, LANES - 1, lane)
    col_first[...] = first
    col_last[...] = last


def plain_gradient_kernel(planes, grad_x, grad_y):
    fields = planes.shape[1]
    ids = lane_ids(fields)
    for q in range(grad_x.shape[0]):
        grad_x[q] = 0.5 * (planes[q + 6] - planes[q + 2])
        plane = planes[q + 4]
        east = jnp.where(ids == LANES - 1, 0.0, pltpu.roll(plane, LANES - 1, 1))
        west = jnp.where(ids == 0, 0.0, pltpu.roll(plane, 1, 1))
        grad_y[q] = 0.5 * (east - west)


def odd_even(packed, ids):
    odd = ids % 2 == 1
    zero = jnp.where(odd, pltpu.roll(packed, 1, 1), packed)
    one = jnp.where(odd, packed, pltpu.roll(packed, LANES - 1, 1))
    return zero, one


def gradient_kernel(extended, left, right, col_first, col_last, grad_x, grad_y, ring, shape):
    fields = extended.shape[1]
    ids = lane_ids(fields)
    from_left = left[...]
    from_right = right[...]
    for q in range(grad_x.shape[0]):
        grad_x[q] = 0.5 * (extended[q + 4] - extended[q])
        plane = extended[q + 2]
        east = put_lane(pltpu.roll(plane, LANES - 1, 1), ids, from_right, q, LANES - 1)
        west = put_lane(pltpu.roll(plane, 1, 1), ids, from_left, q, 0)
        grad_y[q] = 0.5 * (east - west)

    def both(near, far):
        return jnp.where(ids < SIDE, near, pltpu.roll(far, SIDE, 1))

    centre = both(from_left, from_right)
    inner = both(col_first[...], col_last[...])
    outer = pltpu.roll(centre, LANES - SECOND, 1)
    zero, one = odd_even(centre, ids)
    ring[0] = zero
    ring[1] = one
    ring[2] = 0.5 * (pltpu.roll(centre, LANES - 2, 1) - pltpu.roll(centre, 2, 1))
    ring[3] = jnp.where(ids < SIDE, 0.5, -0.5) * (inner - outer)
    ring[4] = centre

    total, count, _ = shape.shape
    beside = centre[0:count, :] * centre[count + 1 : count + 2, :]

    def masked(q):
        return extended[q + 2, 0:count, :] * extended[q + 2, count + 1 : count + 2, :]

    for q in range(total):
        water = extended[q + 4, count + 1 : count + 2, :]
        shape[q] = (TIME_STEP * water) * diffused(masked(q), masked(q + 2), masked(q + 4), beside, q)


def diffused(before, plane, after, beside, q):
    ids = lane_ids(plane.shape[0])
    east = put_lane(pltpu.roll(plane, LANES - 1, 1), ids, beside, q + 2 + SIDE, LANES - 1)
    west = put_lane(pltpu.roll(plane, 1, 1), ids, beside, q + 2, 0)
    return plane + VISCOUS * (before + after + east + west - 4.0 * plane)


def all_tiles(arrays):
    count = arrays[0].shape[0] // TILE * TILE - TILE
    yield from pair_tiles(arrays, count)
    yield from flow_tiles(arrays, count)


def fill_pair_fields(velocity, grads, rows):
    arrays = list(velocity) + [ref for pair in grads for ref in pair]
    for start, leads, parts in all_tiles(arrays):
        for c in range(len(grads)):
            x, y = 2 + 2 * c, 3 + 2 * c
            value = leads[0] * parts[x] + leads[1] * parts[y] + parts[0] * leads[x] + parts[1] * leads[y]
            rows[start : start + TILE, c * LANES : (c + 1) * LANES] = value


def fill_edge_fields(edges, rows):
    for start, leads, parts in all_tiles([ref for edge in edges for ref in edge]):
        for n in range(len(edges)):
            u, d = 2 * n, 2 * n + 1
            value = leads[u] * parts[d] + parts[u] * leads[d]
            rows[start : start + TILE, n * LANES : (n + 1) * LANES] = value


def clear_rest(rows, count):
    used = pair_start(count // TILE) + count
    rows[used:, :] = jnp.zeros((rows.shape[0] - used, rows.shape[1]), jnp.float32)


def add_to_tiles(out, before, stack, rows):
    count = stack.shape[0] // 2
    for first in range(0, rows.shape[0], 2 * LANES):
        last = min(first + 2 * LANES, rows.shape[0])
        value = dot_halves(stack, rows[first:last, :], NT)
        for start in range(first, last, LANES):
            place = slice(start // LANES * count, (start // LANES + 1) * count)
            part = value[:, start - first : start - first + LANES]
            out[place, :] = part if before is None else before[place, :] + part


def tiles_beside(values, count):
    return jnp.concatenate([values[at : at + count, :] for at in range(0, values.shape[0], count)], axis=1)


def tensor_kernel(scale, start, stop, planes, grad_x, grad_y, *refs):
    *before, out, rows = refs
    count = out.shape[0] * LANES // rows.shape[0]
    clear_rest(rows, count)
    out[...] = before[0][...] if before else jnp.zeros(out.shape, jnp.float32)

    def body(x, carry):
        q = 2 * x
        velocity = [planes.at[q + 4], planes.at[q + 5]]
        fill_pair_fields(velocity, [(grad_x.at[q + c], grad_y.at[q + c]) for c in range(2)], rows)
        water = planes[q + 4, count + 1 : count + 2, :] * (-scale)
        weighted = jnp.concatenate([planes[q + 4, 0:count, :] * water, planes[q + 5, 0:count, :] * water], axis=1)
        add_to_tiles(out, out, stacked_halves(weighted), rows)
        return carry

    lax.fori_loop(start, stop, body, 0)


def edge_tensor_kernel(scale, extended, left, right, col_first, col_last, before, out, parts, rows):
    count = out.shape[0] * LANES // rows.shape[0]
    total = extended.shape[0]
    fields = extended.shape[1]
    clear_rest(rows, count)
    ids = lane_ids(fields)
    for c in range(2):
        parts[c] = -0.5 * extended[2 + c]
        parts[2 + c] = 0.5 * extended[total - 4 + c]
    near = (ids >= 2) & (ids < total - 6)
    far = (ids >= 2 + SIDE) & (ids < total - 6 + SIDE)
    parts[4] = jnp.where(near, -0.5 * left[...], jnp.where(far, 0.5 * pltpu.roll(right[...], SIDE, 1), 0.0))
    centre = jnp.where(ids < SIDE, col_first[...], pltpu.roll(col_last[...], SIDE, 1))
    parts[5] = odd_even(centre, ids)[1]
    top, bottom = extended.at[4], extended.at[total - 6]
    fill_edge_fields(
        [
            (top, parts.at[0]), (top, parts.at[1]), (bottom, parts.at[2]), (bottom, parts.at[3]),
            (parts.at[5], parts.at[4]),
        ],
        rows,
    )
    weighted = []
    for plane in (extended[4], extended[5], extended[total - 6], extended[total - 5], centre):
        weighted.append(plane[0:count, :] * (plane[count + 1 : count + 2, :] * (-scale)))
    add_to_tiles(out, before, stacked_halves(jnp.concatenate(weighted, axis=1)), rows)


def inverse_pair(first, second):
    count = first.shape[0]
    row_ids = lax.broadcasted_iota(jnp.int32, (count, count), 0)
    col_ids = lax.broadcasted_iota(jnp.int32, (count, count), 1)
    both = [first, second]
    for k in range(count):
        for n in range(2):
            a = both[n]
            row = a[k : k + 1, :]
            col = a[:, k : k + 1]
            pivot = 1.0 / a[k : k + 1, k : k + 1]
            row = jnp.where(col_ids[0:1] == k, 1.0, row) * pivot
            kept = jnp.where(col_ids == k, 0.0, a)
            both[n] = jnp.where(row_ids == k, row, kept - col * row)
    return both


def inverse_kernel(realizations, early, first, second, share, cov_inverse, gram_inverse, mean, pair_cov, offset):
    count, padded = offset.shape
    packed = jnp.concatenate([early[:, 0:SIDE], early[:, SIDE : 2 * SIDE]], axis=0)
    shared = packed[:, 0:count]
    means = packed[:, count : count + 1] * (1.0 / realizations)
    row_ids = lax.broadcasted_iota(jnp.int32, (count, count), 0)
    col_ids = lax.broadcasted_iota(jnp.int32, (count, count), 1)
    turned = shared.T
    raw_second = jnp.where(col_ids >= row_ids, shared, turned) * (1.0 / realizations)
    gram = jnp.where(col_ids < row_ids, shared, turned)
    gram = jnp.where(col_ids == row_ids, packed[:, count + 1 : count + 2], gram)
    mean_row = jnp.sum(jnp.where(row_ids == col_ids, means, 0.0), axis=0, keepdims=True)
    covariance = raw_second - means * mean_row
    cov_inverse[...], gram_inverse[...] = inverse_pair(covariance, gram)
    ids = lax.broadcasted_iota(jnp.int32, (count, padded), 0)
    pick_first = (ids == first[...]).astype(jnp.float32)
    pick_second = (ids == second[...]).astype(jnp.float32)
    cov_first = dot32(covariance, pick_first, NN)
    cov_second = dot32(covariance, pick_second, NN)
    mean_first = jnp.sum(pick_first * means, axis=0, keepdims=True)
    mean_second = jnp.sum(pick_second * means, axis=0, keepdims=True)
    cov_pair = jnp.sum(pick_first * cov_second, axis=0, keepdims=True)
    offset[...] = means * (cov_pair + mean_first * mean_second) + mean_first * cov_second + mean_second * cov_first
    mean[...] = jnp.broadcast_to(means, mean.shape)
    pair_cov[...] = cov_pair * share[...]


def weight_kernel(realizations, sums, cov_inverse, offset, share, coeffs, mean, weights, pieces, rows):
    count = coeffs.shape[0]
    padded = weights.shape[1]
    pairs = pair_start(count // TILE)
    third = tiles_beside(sums[...], count) * (1.0 / realizations) - offset[...]
    weight_map = dot32(cov_inverse[...], third, NN) * share[...]
    ids = lax.broadcasted_iota(jnp.int32, (count, padded), 0)
    lanes = lax.broadcasted_iota(jnp.int32, (count, padded), 1)
    unit = jnp.where(lanes - pairs == ids, 1.0, 0.0)
    weights[...] = stacked_halves(jnp.where(lanes < pairs, weight_map, unit))
    fill_coeff_rows(coeffs[...] - mean[...], rows)
    pieces[...] = stacked_halves(rows[...])


def forcing_kernel(start, weights, extended, grad_x, grad_y, out, rows):
    count = weights.shape[0] // 2
    clear_rest(rows, count)
    stack = weights[...]

    def body(n, carry):
        q = 2 * (start + n)
        velocity = [extended.at[q + 2], extended.at[q + 3]]
        fill_pair_fields(velocity, [(grad_x.at[q + c], grad_y.at[q + c]) for c in range(2)], rows)
        nonlinear = dot_halves(stack, rows[...], NN)
        water = extended[q + 2, count + 1 : count + 2, :]
        for c in range(2):
            part = nonlinear[:, c * LANES : (c + 1) * LANES]
            out[2 * n + c] = water * (extended[q + 2 + c, 0:count, :] - TIME_STEP * part)
        return carry

    lax.fori_loop(0, out.shape[0] // 2, body, 0)


def ring_forcing_kernel(weights, ring, out, rows):
    count = weights.shape[0] // 2
    clear_rest(rows, count)
    fill_pair_fields([ring.at[0], ring.at[1]], [(ring.at[2], ring.at[3])], rows)
    nonlinear = dot_halves(weights[...], rows[...], NN)
    out[...] = ring[4, count + 1 : count + 2, :] * (ring[4, 0:count, :] - TIME_STEP * nonlinear)


def smooth_kernel(extended, moved, moved_ring, base):
    total, count, _ = base.shape
    beside = moved_ring[...]
    for q in range(total):
        water = extended[q + 4, count + 1 : count + 2, :]
        base[q] = water * diffused(moved[q], moved[q + 2], moved[q + 4], beside, q)


def finish_kernel(
    tensor, weights, pieces, gram_inverse, coeffs, mean, pair_cov, share, base, shape,
    modes_out, coeffs_out, new_modes, new_coeffs, sems,
):
    count = coeffs.shape[0]
    total = base.shape[0]
    inverse = gram_inverse[...]
    tens = tiles_beside(tensor[...], count)
    projected = dot_halves(weights[...], tens, NT)
    stack = stacked_halves(tens * share[...])
    drift = jnp.dot(stack, pieces[0 : tens.shape[1], :], preferred_element_type=jnp.float32)
    drift += jnp.dot(stack, pieces[tens.shape[1] :, :], preferred_element_type=jnp.float32)
    drift = drift[:count] + drift[count:] - jnp.sum(tens * pair_cov[...], axis=1, keepdims=True)
    solved = stacked_halves(dot32(projected, inverse, NN))
    new_coeffs[...] = coeffs[...] - mean[...] + TIME_STEP * dot32(inverse, drift, NN)
    for x in range(total // 2):
        both = jnp.concatenate([shape[2 * x], shape[2 * x + 1]], axis=1)
        change = dot_halves(solved, both, NN)
        for c in range(2):
            value = base[2 * x + c] - change[:, c * LANES : (c + 1) * LANES]
            new_modes[pl.ds(c * (total // 2) + x, count, stride=total), :] = value
    leaving = [
        pltpu.make_async_copy(new_coeffs, coeffs_out, sems.at[0]),
        pltpu.make_async_copy(new_modes, modes_out, sems.at[1]),
    ]
    for leave in leaving:
        leave.start()
    for leave in leaving:
        leave.wait()


def axis_bits(axis):
    count = lax.axis_size(axis)
    assert count & (count - 1) == 0
    return list(range(count.bit_length() - 1))


def swap(values, axis, partner):
    return lax.ppermute(values, axis, list(enumerate(partner)))


def pairs_a(axis):
    return [i ^ 1 for i in range(lax.axis_size(axis))]


def shifted(axis, distance):
    count = lax.axis_size(axis)
    return [(((i - 1) % count ^ distance) + 1) % count for i in range(count)]


def later_steps(axis):
    return [(axis, shifted(axis, 1 << bit)) for bit in axis_bits(axis)[2:]]


def with_edges(axis, partner, values, *edges):
    rows = [values.shape[0]] + [edge.shape[0] * edge.shape[1] for edge in edges]
    flat = [values] + [edge.reshape(-1, edge.shape[-1]) for edge in edges]
    arrived = swap(jnp.concatenate(flat, axis=0), axis, partner)
    ends = np.cumsum(rows)
    return [arrived[: rows[0]]] + [
        arrived[ends[n] : ends[n + 1]].reshape(edge.shape) for n, edge in enumerate(edges)
    ]


def neighbours(axis, from_a, from_b):
    here = lax.axis_index(axis)
    even = here % 2 == 0
    before = jnp.where(here == 0, 0.0, jnp.where(even, from_b, from_a))
    after = jnp.where(here == lax.axis_size(axis) - 1, 0.0, jnp.where(even, from_a, from_b))
    return before, after


def split(values, lower):
    half = values.shape[0] // 2
    top, bottom = values[:half], values[half:]
    return jnp.where(lower, top, bottom), jnp.where(lower, bottom, top)


def joined(kept, other, lower):
    return jnp.concatenate([jnp.where(lower, kept, other), jnp.where(lower, other, kept)], axis=0)


def tied(*values):
    return lax.optimization_barrier(values)


def shape32(*dims):
    return jax.ShapeDtypeStruct(dims, jnp.float32)


def vmem32(*dims):
    return pltpu.VMEM(dims, jnp.float32)


PARAMS = pltpu.CompilerParams(vmem_limit_bytes=32 * 1024 * 1024)


def on_device(modes, mean_flow, seeds, amplitudes, water_mask):
    count, _, nx, ny = modes.shape
    devices = lax.axis_size("row") * lax.axis_size("col")
    rows_dev = seeds.shape[0]
    row_total = rows_dev * devices
    scale = 1.0 / (2.0 * nx * ny * devices)
    pairs, padded, first, second, share = pair_layout(count)
    tiles = padded // LANES
    fields = count + TILE
    total = 2 * (nx + 4)
    assert ny == LANES and 2 * (nx + 2) <= SECOND and count % (2 * TILE) == 0
    call = functools.partial(pl.pallas_call, compiler_params=PARAMS)
    assert min(lax.axis_size("row"), lax.axis_size("col")) >= 4

    first_row = lax.axis_index(("row", "col")) * rows_dev
    row_ids = (first_row + jnp.arange(rows_dev, dtype=jnp.int32)).astype(jnp.float32)
    strength = (0.5 + row_ids / row_total).reshape(1, rows_dev)
    planes, own_first, own_last, sums, early, coeffs = call(
        functools.partial(front_kernel, scale),
        out_shape=(
            shape32(total, fields, ny), shape32(fields, ny), shape32(fields, ny),
            shape32(tiles * count, LANES), shape32(count // 2, LANES), shape32(count, rows_dev),
        ),
        scratch_shapes=[vmem32(padded, rows_dev)],
    )(
        modes.reshape(count * 2 * nx, ny), mean_flow.reshape(2 * nx, ny), water_mask, seeds.T,
        strength, amplitudes.reshape(1, count),
    )

    grads = call(
        plain_gradient_kernel, out_shape=(shape32(2 * nx, fields, ny), shape32(2 * nx, fields, ny))
    )(planes)

    def tensor_piece(number, grads, *before):
        start, stop = nx * number // 3, nx * (number + 1) // 3
        return call(
            functools.partial(tensor_kernel, scale, start, stop),
            out_shape=shape32(tiles * count, LANES),
            scratch_shapes=[vmem32(padded, 2 * ny)],
        )(planes, *grads, *before)

    top, bottom = planes[4:8], planes[total - 8 : total - 4]
    row, col = lax.axis_index("row"), lax.axis_index("col")
    even_row, even_col = row % 2 == 0, col % 2 == 0
    lower_a, lower_b = (row + 1) // 2 % 2 == 0, row % 2 == 1
    row_a, row_b = pairs_a("row"), shifted("row", 1)
    col_a, col_b = pairs_a("col"), shifted("col", 1)

    kept, sent = split(sums, lower_a)
    arrived, extra, row_from_a = with_edges("row", row_a, sent, early[None], jnp.where(even_row, bottom, top))
    kept, early, grads = tied(kept + arrived, early + extra[0], grads)
    kept, sent = split(kept, lower_b)
    arrived, extra, row_from_b = with_edges("row", row_b, sent, early[None], jnp.where(even_row, top, bottom))
    above, below = neighbours("row", row_from_a, row_from_b)
    tensor = tensor_piece(0, grads)
    kept, early, above, below, tensor = tied(kept + arrived, early + extra[0], above, below, tensor)
    extended, col_first, col_last = call(
        extend_kernel,
        out_shape=(shape32(total, fields, ny), shape32(fields, ny), shape32(fields, ny)),
    )(planes, above, below, own_first, own_last)
    first_edge, last_edge = col_first[None], col_last[None]
    arrived, extra, col_from_a = with_edges("col", col_a, kept, early[None], jnp.where(even_col, last_edge, first_edge))
    tensor = tensor_piece(1, grads, tensor)
    kept, early, tensor = tied(kept + arrived, early + extra[0], tensor)
    arrived, extra, col_from_b = with_edges("col", col_b, kept, early[None], jnp.where(even_col, first_edge, last_edge))
    left, right = (edge[0] for edge in neighbours("col", col_from_a, col_from_b))
    tensor = tensor_piece(2, grads, tensor)
    kept, early, left, right, tensor = tied(kept + arrived, early + extra[0], left, right, tensor)

    later = later_steps("row") + later_steps("col")
    for number, (axis, partner) in enumerate(later):
        arrived, extra = with_edges(axis, partner, kept, early[None])
        kept, early = kept + arrived, early + extra[0]
        if number == 0:
            tensor = call(
                functools.partial(edge_tensor_kernel, scale),
                out_shape=shape32(tiles * count, LANES),
                scratch_shapes=[vmem32(6, fields, ny), vmem32(padded, 5 * ny)],
            )(extended, left, right, col_first, col_last, tensor)
            grad_x, grad_y, ring, shape = call(
                gradient_kernel,
                out_shape=(
                    shape32(total - 4, fields, ny), shape32(total - 4, fields, ny), shape32(5, fields, ny),
                    shape32(2 * nx, count, ny),
                ),
            )(extended, left, right, col_first, col_last)
        kept, early, tensor, shape = tied(kept, early, tensor, shape)
    moments = kept

    kept, sent = split(tensor, lower_a)
    kept, moments = tied(kept + swap(sent, "row", row_a), moments)
    kept, sent = split(kept, lower_b)
    arrived, other = with_edges("row", row_b, sent, moments[None])
    kept = kept + arrived
    cov_inverse, gram_inverse, mean, pair_cov, offset = call(
        functools.partial(inverse_kernel, row_total),
        out_shape=(
            shape32(count, count), shape32(count, count), shape32(count, rows_dev), shape32(1, padded),
            shape32(count, padded),
        ),
    )(early, first, second, share)
    moments = joined(moments, other[0], lower_b)
    kept, moments, offset = tied(kept, moments, offset)
    sums = joined(moments, swap(moments, "row", row_a), lower_a)
    kept, sums = tied(kept, sums)
    weights, pieces = call(
        functools.partial(weight_kernel, row_total),
        out_shape=(
            jax.ShapeDtypeStruct((2 * count, padded), jnp.bfloat16),
            jax.ShapeDtypeStruct((2 * padded, rows_dev), jnp.bfloat16),
        ),
        scratch_shapes=[vmem32(padded, rows_dev)],
    )(sums, cov_inverse, offset, share, coeffs, mean)
    col_bits = axis_bits("col")
    steps = later_steps("row") + [
        ("col", [i ^ (1 << bit) for i in range(lax.axis_size("col"))]) for bit in col_bits[-1:] + col_bits[:-1]
    ]

    def forcing(start, stop):
        return call(
            functools.partial(forcing_kernel, start),
            out_shape=shape32(2 * (stop - start), count, ny),
            scratch_shapes=[vmem32(padded, 2 * ny)],
        )(weights, extended, grad_x, grad_y)

    def ring_forcing():
        return call(ring_forcing_kernel, out_shape=shape32(count, ny), scratch_shapes=[vmem32(padded, ny)])(
            weights, ring
        )

    ends = [(nx + 2) * n // 10 for n in (0, 4, 7, 10)]
    works = [functools.partial(forcing, ends[n], ends[n + 1]) for n in range(3)] + [ring_forcing]
    moved = []
    for axis, partner in steps:
        total_kept = kept + swap(kept, axis, partner)
        if works:
            moved.append(works.pop(0)())
        kept, weights, moved = tied(total_kept, weights, moved)
    kept = joined(kept, swap(kept, "row", row_b), lower_b)
    while works:
        moved.append(works.pop(0)())
    base = call(smooth_kernel, out_shape=shape32(2 * nx, count, ny))(
        extended, jnp.concatenate(moved[:-1], axis=0), moved[-1]
    )
    kept, base = tied(kept, base)
    tensor = joined(kept, swap(kept, "row", row_a), lower_a)

    new_modes, new_coeffs = call(
        finish_kernel,
        out_shape=(shape32(count * 2 * nx, ny), shape32(count, rows_dev)),
        out_specs=(pl.BlockSpec(memory_space=pltpu.HBM),) * 2,
        scratch_shapes=[vmem32(count * 2 * nx, ny), vmem32(count, rows_dev), pltpu.SemaphoreType.DMA((2,))],
    )(tensor, weights, pieces, gram_inverse, coeffs, mean, pair_cov, share, base, shape)
    return (new_modes.reshape(modes.shape), new_coeffs.T)


def solution(mesh):
    return jax.shard_map(
        on_device,
        mesh=mesh,
        in_specs=(
            P(None, None, "row", "col"),
            P(None, "row", "col"),
            P(("row", "col"), None),
            P(),
            P("row", "col"),
        ),
        out_specs=(P(None, None, "row", "col"), P(("row", "col"), None)),
        check_vma=False,
    )
```

```python
import functools
import math

import jax
import jax.numpy as jnp
import numpy as np
from jax import lax
from jax.experimental import pallas as pl
from jax.experimental.pallas import tpu as pltpu
from jax.sharding import PartitionSpec as P

TIME_STEP = 0.25
VISCOUS = 0.2
PRECISE = lax.Precision.HIGHEST
TILE = 8
LANES = 128
NT = (((1,), (1,)), ((), ()))
NN = (((1,), (0,)), ((), ()))


HALF_TILE = TILE // 2


def pair_start(block):
    return TILE * (TILE * block * (block - 1) // 2 + (HALF_TILE + 1) * block)


def pair_layout(count):
    blocks = count // TILE
    pairs = pair_start(blocks)
    padded = -(-(pairs + count + 2) // LANES) * LANES
    first = np.full((1, padded), -1, np.int32)
    second = np.full((1, padded), -1, np.int32)
    share = np.zeros((1, padded), np.float32)

    def put(row, j, k):
        first[0, row], second[0, row], share[0, row] = j, k, 0.5 if j == k else 1.0

    for block in range(blocks):
        row = pair_start(block)
        base = TILE * block
        for j in range(base):
            for r in range(TILE):
                put(row + TILE * j + r, j, base + r)
        row += TILE * base
        for n in range(HALF_TILE + 1):
            for r in range(TILE):
                if r >= n:
                    put(row + TILE * n + r, base + n, base + r)
                elif n < HALF_TILE:
                    put(row + TILE * n + r, base + TILE - n, base + TILE - n + r)
    share[0, pairs : pairs + count] = 1.0
    return pairs, padded, first, second, share


def pair_tiles(arrays, count):
    blocks = count // TILE
    ids = lax.broadcasted_iota(jnp.int32, (TILE, arrays[0].shape[1]), 0)

    def tile(block):
        return [a[TILE * block : TILE * block + TILE, :] for a in arrays]

    for j in range(count):
        leads = [a[j : j + 1, :] for a in arrays]
        for block in range(j // TILE + 1, blocks):
            yield pair_start(block) + TILE * j, leads, tile(block)
    for block in range(blocks):
        base = TILE * block
        for n in range(HALF_TILE + 1):
            leads, parts = [a[base + n : base + n + 1, :] for a in arrays], tile(block)
            if 0 < n < HALF_TILE:
                other = base + TILE - n
                leads = [jnp.where(ids < n, a[other : other + 1, :], lead) for a, lead in zip(arrays, leads)]
                parts = [jnp.where(ids < n, pltpu.roll(part, n, 0), part) for part in parts]
            yield pair_start(block) + TILE * (base + n), leads, parts


def flow_tiles(arrays, count):
    leads = [a[count : count + 1, :] for a in arrays]
    for block in range(count // TILE):
        rows = slice(TILE * block, TILE * block + TILE)
        yield pair_start(count // TILE) + TILE * block, leads, [a[rows, :] for a in arrays]


def dot32(left, right, dims):
    return lax.dot_general(left, right, dims, precision=PRECISE, preferred_element_type=jnp.float32)


def halves(values):
    high = values.astype(jnp.bfloat16)
    low = (values - high.astype(jnp.float32)).astype(jnp.bfloat16)
    return high, low


def stacked_halves(values):
    high, low = halves(values)
    return jnp.concatenate([high, low], axis=0)


def dot_halves(left_stack, right, dims):
    high, low = halves(right)
    both = lax.dot_general(left_stack, high, dims, preferred_element_type=jnp.float32)
    both += lax.dot_general(left_stack, low, dims, preferred_element_type=jnp.float32)
    rows = left_stack.shape[0] // 2
    return both[:rows] + both[rows:]


def lane_ids(rows):
    return lax.broadcasted_iota(jnp.int32, (rows, LANES), 1)


SECOND = 32
SIDE = 64


def put_lane(packed, ids, plane, lane, target):
    return jnp.where(ids == target, pltpu.roll(plane, (target - lane) % LANES, 1), packed)


def front_kernel(
    scale, modes, flow, water, seeds, strength, amplitudes, planes, sums, early, coeffs, rows
):
    step = coeffs.shape[0]
    total = modes.shape[0] // step
    nx = total // 2
    planes[...] = jnp.zeros(planes.shape, jnp.float32)
    diagonal = lax.broadcasted_iota(jnp.int32, (step, step), 0) == lax.broadcasted_iota(jnp.int32, (step, step), 1)
    heights = jnp.sum(jnp.where(diagonal, amplitudes[...], 0.0), axis=1, keepdims=True)
    wave = jnp.cos(seeds[...].astype(jnp.float32) * (3.0 * math.pi / 8192.0))
    values = strength[...] * heights * (wave + (wave * wave - 0.5))
    coeffs[...] = values
    pairs = pair_start(step // TILE)
    fill_coeff_rows(values, rows)
    rows[pairs + step : pairs + step + 1, :] = jnp.ones((1, values.shape[1]), jnp.float32)
    moments = dot32(values, rows[...], NT)
    tiles = moments.shape[1] // LANES
    for tile in range(tiles):
        sums[tile * step : (tile + 1) * step, :] = moments[:, tile * LANES : (tile + 1) * LANES]
    gram = jnp.zeros((step, step), jnp.float32)
    for x in range(nx):
        mask = water[x : x + 1, :].astype(jnp.float32)
        both = []
        for c in range(2):
            q = 2 * x + c
            field = modes[pl.ds(c * nx + x, step, stride=total), :]
            both.append(field)
            planes[q + 4, 0:step, :] = field
            planes[q + 4, step : step + 1, :] = flow[c * nx + x : c * nx + x + 1, :]
            planes[q + 4, step + 1 : step + 2, :] = mask
        wide = jnp.concatenate(both, axis=1)
        weight = jnp.concatenate([mask, mask], axis=1) * scale
        gram += dot_halves(stacked_halves(wide * weight), wide, NT)
    heads = lax.broadcasted_iota(jnp.int32, (step, step), 0)
    lanes = lax.broadcasted_iota(jnp.int32, (step, step), 1)
    both = jnp.where(lanes < heads, gram, moments[:, pairs : pairs + step])
    corner = jnp.sum(jnp.where(lanes == heads, gram, 0.0), axis=1, keepdims=True)
    rest = jnp.zeros((step, SIDE - step - 2), jnp.float32)
    packed = jnp.concatenate([both, moments[:, pairs + step : pairs + step + 1], corner, rest], axis=1)
    early[...] = jnp.concatenate([packed[: step // 2], packed[step // 2 :]], axis=1)


def fill_coeff_rows(values, rows):
    count = values.shape[0]
    pairs = pair_start(count // TILE)
    for start, (lead,), (part,) in pair_tiles([values], count):
        rows[start : start + TILE, :] = lead * part
    rows[pairs : pairs + count, :] = values
    rows[pairs + count :, :] = jnp.zeros((rows.shape[0] - pairs - count, values.shape[1]), jnp.float32)


def extend_kernel(planes, above, below, first_in, last_in, extended, col_first, col_last):
    total = planes.shape[0]
    fields = planes.shape[1]
    ids = lane_ids(fields)
    extended[...] = planes[...]
    extended[2:4] = above[...]
    extended[total - 4 : total - 2] = below[...]
    first = first_in[...]
    last = last_in[...]
    for c in range(2):
        for plane, lane in ((above[c], c), (below[c], total - 6 + c)):
            first = put_lane(first, ids, plane, 0, lane)
            last = put_lane(last, ids, plane, LANES - 1, lane)
    col_first[...] = first
    col_last[...] = last


def plain_gradient_kernel(planes, grad_x, grad_y, col_first, col_last):
    fields = planes.shape[1]
    ids = lane_ids(fields)
    first = jnp.zeros((fields, LANES), jnp.float32)
    last = jnp.zeros((fields, LANES), jnp.float32)
    for q in range(grad_x.shape[0]):
        grad_x[q] = 0.5 * (planes[q + 6] - planes[q + 2])
        plane = planes[q + 4]
        east = jnp.where(ids == LANES - 1, 0.0, pltpu.roll(plane, LANES - 1, 1))
        west = jnp.where(ids == 0, 0.0, pltpu.roll(plane, 1, 1))
        grad_y[q] = 0.5 * (east - west)
        first = put_lane(first, ids, plane, 0, q + 2)
        first = put_lane(first, ids, plane, 1, q + 2 + SECOND)
        last = put_lane(last, ids, plane, LANES - 1, q + 2)
        last = put_lane(last, ids, plane, LANES - 2, q + 2 + SECOND)
    col_first[...] = first
    col_last[...] = last


def odd_even(packed, ids):
    odd = ids % 2 == 1
    zero = jnp.where(odd, pltpu.roll(packed, 1, 1), packed)
    one = jnp.where(odd, packed, pltpu.roll(packed, LANES - 1, 1))
    return zero, one


def gradient_kernel(extended, left, right, col_first, col_last, grad_x, grad_y, ring, shape):
    fields = extended.shape[1]
    ids = lane_ids(fields)
    from_left = left[...]
    from_right = right[...]
    for q in range(grad_x.shape[0]):
        grad_x[q] = 0.5 * (extended[q + 4] - extended[q])
        plane = extended[q + 2]
        east = put_lane(pltpu.roll(plane, LANES - 1, 1), ids, from_right, q, LANES - 1)
        west = put_lane(pltpu.roll(plane, 1, 1), ids, from_left, q, 0)
        grad_y[q] = 0.5 * (east - west)

    def both(near, far):
        return jnp.where(ids < SIDE, near, pltpu.roll(far, SIDE, 1))

    centre = both(from_left, from_right)
    inner = both(col_first[...], col_last[...])
    outer = pltpu.roll(centre, LANES - SECOND, 1)
    zero, one = odd_even(centre, ids)
    ring[0] = zero
    ring[1] = one
    ring[2] = 0.5 * (pltpu.roll(centre, LANES - 2, 1) - pltpu.roll(centre, 2, 1))
    ring[3] = jnp.where(ids < SIDE, 0.5, -0.5) * (inner - outer)
    ring[4] = centre

    total, count, _ = shape.shape
    beside = centre[0:count, :] * centre[count + 1 : count + 2, :]

    def masked(q):
        return extended[q + 2, 0:count, :] * extended[q + 2, count + 1 : count + 2, :]

    for q in range(total):
        water = extended[q + 4, count + 1 : count + 2, :]
        shape[q] = (TIME_STEP * water) * diffused(masked(q), masked(q + 2), masked(q + 4), beside, q)


def diffused(before, plane, after, beside, q):
    ids = lane_ids(plane.shape[0])
    east = put_lane(pltpu.roll(plane, LANES - 1, 1), ids, beside, q + 2 + SIDE, LANES - 1)
    west = put_lane(pltpu.roll(plane, 1, 1), ids, beside, q + 2, 0)
    return plane + VISCOUS * (before + after + east + west - 4.0 * plane)


def all_tiles(arrays):
    count = arrays[0].shape[0] // TILE * TILE - TILE
    yield from pair_tiles(arrays, count)
    yield from flow_tiles(arrays, count)


def fill_pair_fields(velocity, grads, rows):
    arrays = list(velocity) + [ref for pair in grads for ref in pair]
    for start, leads, parts in all_tiles(arrays):
        for c in range(len(grads)):
            x, y = 2 + 2 * c, 3 + 2 * c
            value = leads[0] * parts[x] + leads[1] * parts[y] + parts[0] * leads[x] + parts[1] * leads[y]
            rows[start : start + TILE, c * LANES : (c + 1) * LANES] = value


def fill_edge_fields(edges, rows):
    for start, leads, parts in all_tiles([ref for edge in edges for ref in edge]):
        for n in range(len(edges)):
            u, d = 2 * n, 2 * n + 1
            value = leads[u] * parts[d] + parts[u] * leads[d]
            rows[start : start + TILE, n * LANES : (n + 1) * LANES] = value


def clear_rest(rows, count):
    used = pair_start(count // TILE) + count
    rows[used:, :] = jnp.zeros((rows.shape[0] - used, rows.shape[1]), jnp.float32)


def add_to_tiles(out, before, stack, rows):
    count = stack.shape[0] // 2
    for first in range(0, rows.shape[0], 2 * LANES):
        last = min(first + 2 * LANES, rows.shape[0])
        value = dot_halves(stack, rows[first:last, :], NT)
        for start in range(first, last, LANES):
            place = slice(start // LANES * count, (start // LANES + 1) * count)
            part = value[:, start - first : start - first + LANES]
            out[place, :] = part if before is None else before[place, :] + part


def tiles_beside(values, count):
    return jnp.concatenate([values[at : at + count, :] for at in range(0, values.shape[0], count)], axis=1)


def tensor_kernel(scale, start, stop, planes, grad_x, grad_y, *refs):
    *before, out, rows = refs
    count = out.shape[0] * LANES // rows.shape[0]
    clear_rest(rows, count)
    out[...] = before[0][...] if before else jnp.zeros(out.shape, jnp.float32)

    def body(x, carry):
        q = 2 * x
        velocity = [planes.at[q + 4], planes.at[q + 5]]
        fill_pair_fields(velocity, [(grad_x.at[q + c], grad_y.at[q + c]) for c in range(2)], rows)
        water = planes[q + 4, count + 1 : count + 2, :] * (-scale)
        weighted = jnp.concatenate([planes[q + 4, 0:count, :] * water, planes[q + 5, 0:count, :] * water], axis=1)
        add_to_tiles(out, out, stacked_halves(weighted), rows)
        return carry

    lax.fori_loop(start, stop, body, 0)


def edge_tensor_kernel(scale, extended, left, right, col_first, col_last, before, out, parts, rows):
    count = out.shape[0] * LANES // rows.shape[0]
    total = extended.shape[0]
    fields = extended.shape[1]
    clear_rest(rows, count)
    ids = lane_ids(fields)
    for c in range(2):
        parts[c] = -0.5 * extended[2 + c]
        parts[2 + c] = 0.5 * extended[total - 4 + c]
    near = (ids >= 2) & (ids < total - 6)
    far = (ids >= 2 + SIDE) & (ids < total - 6 + SIDE)
    parts[4] = jnp.where(near, -0.5 * left[...], jnp.where(far, 0.5 * pltpu.roll(right[...], SIDE, 1), 0.0))
    centre = jnp.where(ids < SIDE, col_first[...], pltpu.roll(col_last[...], SIDE, 1))
    parts[5] = odd_even(centre, ids)[1]
    top, bottom = extended.at[4], extended.at[total - 6]
    fill_edge_fields(
        [
            (top, parts.at[0]), (top, parts.at[1]), (bottom, parts.at[2]), (bottom, parts.at[3]),
            (parts.at[5], parts.at[4]),
        ],
        rows,
    )
    weighted = []
    for plane in (extended[4], extended[5], extended[total - 6], extended[total - 5], centre):
        weighted.append(plane[0:count, :] * (plane[count + 1 : count + 2, :] * (-scale)))
    add_to_tiles(out, before, stacked_halves(jnp.concatenate(weighted, axis=1)), rows)


def inverse_pair(first, second):
    count = first.shape[0]
    row_ids = lax.broadcasted_iota(jnp.int32, (count, count), 0)
    col_ids = lax.broadcasted_iota(jnp.int32, (count, count), 1)
    both = [first, second]
    for k in range(count):
        for n in range(2):
            a = both[n]
            row = a[k : k + 1, :]
            col = a[:, k : k + 1]
            pivot = 1.0 / a[k : k + 1, k : k + 1]
            row = jnp.where(col_ids[0:1] == k, 1.0, row) * pivot
            kept = jnp.where(col_ids == k, 0.0, a)
            both[n] = jnp.where(row_ids == k, row, kept - col * row)
    return both


def offset_kernel(realizations, early, first, second, share, both, mean, pair_cov, offset):
    count, padded = offset.shape
    packed = jnp.concatenate([early[:, 0:SIDE], early[:, SIDE : 2 * SIDE]], axis=0)
    shared = packed[:, 0:count]
    means = packed[:, count : count + 1] * (1.0 / realizations)
    row_ids = lax.broadcasted_iota(jnp.int32, (count, count), 0)
    col_ids = lax.broadcasted_iota(jnp.int32, (count, count), 1)
    turned = shared.T
    raw_second = jnp.where(col_ids >= row_ids, shared, turned) * (1.0 / realizations)
    gram = jnp.where(col_ids < row_ids, shared, turned)
    gram = jnp.where(col_ids == row_ids, packed[:, count + 1 : count + 2], gram)
    mean_row = jnp.sum(jnp.where(row_ids == col_ids, means, 0.0), axis=0, keepdims=True)
    covariance = raw_second - means * mean_row
    both[0] = covariance
    both[1] = gram
    ids = lax.broadcasted_iota(jnp.int32, (count, padded), 0)
    pick_first = (ids == first[...]).astype(jnp.float32)
    pick_second = (ids == second[...]).astype(jnp.float32)
    cov_first = dot32(covariance, pick_first, NN)
    cov_second = dot32(covariance, pick_second, NN)
    mean_first = jnp.sum(pick_first * means, axis=0, keepdims=True)
    mean_second = jnp.sum(pick_second * means, axis=0, keepdims=True)
    cov_pair = jnp.sum(pick_first * cov_second, axis=0, keepdims=True)
    offset[...] = means * (cov_pair + mean_first * mean_second) + mean_first * cov_second + mean_second * cov_first
    mean[...] = jnp.broadcast_to(means, mean.shape)
    pair_cov[...] = cov_pair * share[...]


def inverse_kernel(both, cov_inverse, gram_inverse):
    cov_inverse[...], gram_inverse[...] = inverse_pair(both[0], both[1])


def weight_kernel(realizations, sums, cov_inverse, offset, share, coeffs, mean, weights, pieces, rows):
    count = coeffs.shape[0]
    padded = weights.shape[1]
    pairs = pair_start(count // TILE)
    third = tiles_beside(sums[...], count) * (1.0 / realizations) - offset[...]
    weight_map = dot32(cov_inverse[...], third, NN) * share[...]
    ids = lax.broadcasted_iota(jnp.int32, (count, padded), 0)
    lanes = lax.broadcasted_iota(jnp.int32, (count, padded), 1)
    unit = jnp.where(lanes - pairs == ids, 1.0, 0.0)
    weights[...] = stacked_halves(jnp.where(lanes < pairs, weight_map, unit))
    fill_coeff_rows(coeffs[...] - mean[...], rows)
    pieces[...] = stacked_halves(rows[...])


def forcing_kernel(start, weights, extended, grad_x, grad_y, out, rows):
    count = weights.shape[0] // 2
    clear_rest(rows, count)
    stack = weights[...]

    def body(n, carry):
        q = 2 * (start + n)
        velocity = [extended.at[q + 2], extended.at[q + 3]]
        fill_pair_fields(velocity, [(grad_x.at[q + c], grad_y.at[q + c]) for c in range(2)], rows)
        nonlinear = dot_halves(stack, rows[...], NN)
        water = extended[q + 2, count + 1 : count + 2, :]
        for c in range(2):
            part = nonlinear[:, c * LANES : (c + 1) * LANES]
            out[2 * n + c] = water * (extended[q + 2 + c, 0:count, :] - TIME_STEP * part)
        return carry

    lax.fori_loop(0, out.shape[0] // 2, body, 0)


def ring_forcing_kernel(weights, extended, far_above, far_below, grad_y, ring, out_rows, out, edge_x, rows):
    count = weights.shape[0] // 2
    total = extended.shape[0]
    clear_rest(rows, count)
    stack = weights[...]
    for c in range(2):
        edge_x[c] = 0.5 * (extended[4 + c] - far_above[c])
        edge_x[2 + c] = 0.5 * (far_below[c] - extended[total - 6 + c])

    def body(n, carry):
        q = n * (total - 6)
        velocity = [extended.at[q + 2], extended.at[q + 3]]
        fill_pair_fields(velocity, [(edge_x.at[2 * n + c], grad_y.at[q + c]) for c in range(2)], rows)
        nonlinear = dot_halves(stack, rows[...], NN)
        water = extended[q + 2, count + 1 : count + 2, :]
        for c in range(2):
            part = nonlinear[:, c * LANES : (c + 1) * LANES]
            out_rows[2 * n + c] = water * (extended[q + 2 + c, 0:count, :] - TIME_STEP * part)
        return carry

    lax.fori_loop(0, 2, body, 0)
    fill_pair_fields([ring.at[0], ring.at[1]], [(ring.at[2], ring.at[3])], rows)
    nonlinear = dot_halves(stack, rows[:, :LANES], NN)
    out[...] = ring[4, count + 1 : count + 2, :] * (ring[4, 0:count, :] - TIME_STEP * nonlinear)


def smooth_kernel(extended, moved, moved_ring, base):
    total, count, _ = base.shape
    beside = moved_ring[...]
    for q in range(total):
        water = extended[q + 4, count + 1 : count + 2, :]
        base[q] = water * diffused(moved[q], moved[q + 2], moved[q + 4], beside, q)


def finish_kernel(
    tensor, weights, pieces, gram_inverse, coeffs, mean, pair_cov, share, base, shape,
    modes_out, coeffs_out, new_modes, new_coeffs, sems,
):
    count = coeffs.shape[0]
    total = base.shape[0]
    inverse = gram_inverse[...]
    tens = tiles_beside(tensor[...], count)
    projected = dot_halves(weights[...], tens, NT)
    stack = stacked_halves(tens * share[...])
    drift = jnp.dot(stack, pieces[0 : tens.shape[1], :], preferred_element_type=jnp.float32)
    drift += jnp.dot(stack, pieces[tens.shape[1] :, :], preferred_element_type=jnp.float32)
    drift = drift[:count] + drift[count:] - jnp.sum(tens * pair_cov[...], axis=1, keepdims=True)
    solved = stacked_halves(dot32(projected, inverse, NN))
    new_coeffs[...] = coeffs[...] - mean[...] + TIME_STEP * dot32(inverse, drift, NN)
    for x in range(total // 2):
        both = jnp.concatenate([shape[2 * x], shape[2 * x + 1]], axis=1)
        change = dot_halves(solved, both, NN)
        for c in range(2):
            value = base[2 * x + c] - change[:, c * LANES : (c + 1) * LANES]
            new_modes[pl.ds(c * (total // 2) + x, count, stride=total), :] = value
    leaving = [
        pltpu.make_async_copy(new_coeffs, coeffs_out, sems.at[0]),
        pltpu.make_async_copy(new_modes, modes_out, sems.at[1]),
    ]
    for leave in leaving:
        leave.start()
    for leave in leaving:
        leave.wait()


def axis_bits(axis):
    count = lax.axis_size(axis)
    assert count & (count - 1) == 0
    return list(range(count.bit_length() - 1))


def swap(values, axis, partner):
    return lax.ppermute(values, axis, list(enumerate(partner)))


def pairs_a(axis):
    return [i ^ 1 for i in range(lax.axis_size(axis))]


def shifted(axis, distance):
    count = lax.axis_size(axis)
    return [(((i - 1) % count ^ distance) + 1) % count for i in range(count)]


def later_steps(axis):
    return [(axis, shifted(axis, 1 << bit)) for bit in axis_bits(axis)[2:]]


def with_edges(axis, partner, values, *edges):
    rows = [values.shape[0]] + [edge.shape[0] * edge.shape[1] for edge in edges]
    flat = [values] + [edge.reshape(-1, edge.shape[-1]) for edge in edges]
    arrived = swap(jnp.concatenate(flat, axis=0), axis, partner)
    ends = np.cumsum(rows)
    return [arrived[: rows[0]]] + [
        arrived[ends[n] : ends[n + 1]].reshape(edge.shape) for n, edge in enumerate(edges)
    ]


def neighbours(axis, from_a, from_b):
    here = lax.axis_index(axis)
    even = here % 2 == 0
    before = jnp.where(here == 0, 0.0, jnp.where(even, from_b, from_a))
    after = jnp.where(here == lax.axis_size(axis) - 1, 0.0, jnp.where(even, from_a, from_b))
    return before, after


def split(values, lower):
    half = values.shape[0] // 2
    top, bottom = values[:half], values[half:]
    return jnp.where(lower, top, bottom), jnp.where(lower, bottom, top)


def joined(kept, other, lower):
    return jnp.concatenate([jnp.where(lower, kept, other), jnp.where(lower, other, kept)], axis=0)


def tied(*values):
    return lax.optimization_barrier(values)


def shape32(*dims):
    return jax.ShapeDtypeStruct(dims, jnp.float32)


def vmem32(*dims):
    return pltpu.VMEM(dims, jnp.float32)


PARAMS = pltpu.CompilerParams(vmem_limit_bytes=32 * 1024 * 1024)


def on_device(modes, mean_flow, seeds, amplitudes, water_mask):
    count, _, nx, ny = modes.shape
    devices = lax.axis_size("row") * lax.axis_size("col")
    rows_dev = seeds.shape[0]
    row_total = rows_dev * devices
    scale = 1.0 / (2.0 * nx * ny * devices)
    pairs, padded, first, second, share = pair_layout(count)
    tiles = padded // LANES
    fields = count + TILE
    total = 2 * (nx + 4)
    assert ny == LANES and 2 * (nx + 2) <= SECOND and count % (2 * TILE) == 0
    call = functools.partial(pl.pallas_call, compiler_params=PARAMS)
    assert min(lax.axis_size("row"), lax.axis_size("col")) >= 4

    first_row = lax.axis_index(("row", "col")) * rows_dev
    row_ids = (first_row + jnp.arange(rows_dev, dtype=jnp.int32)).astype(jnp.float32)
    strength = (0.5 + row_ids / row_total).reshape(1, rows_dev)
    planes, sums, early, coeffs = call(
        functools.partial(front_kernel, scale),
        out_shape=(
            shape32(total, fields, ny), shape32(tiles * count, LANES), shape32(count // 2, LANES),
            shape32(count, rows_dev),
        ),
        scratch_shapes=[vmem32(padded, rows_dev)],
    )(
        modes.reshape(count * 2 * nx, ny), mean_flow.reshape(2 * nx, ny), water_mask, seeds.T,
        strength, amplitudes.reshape(1, count),
    )

    *grads, own_first, own_last = call(
        plain_gradient_kernel,
        out_shape=(
            shape32(2 * nx, fields, ny), shape32(2 * nx, fields, ny), shape32(fields, ny), shape32(fields, ny),
        ),
    )(planes)

    def tensor_piece(number, grads, *before):
        start, stop = nx * number // 3, nx * (number + 1) // 3
        return call(
            functools.partial(tensor_kernel, scale, start, stop),
            out_shape=shape32(tiles * count, LANES),
            scratch_shapes=[vmem32(padded, 2 * ny)],
        )(planes, *grads, *before)

    near_top, far_top = planes[4:6], planes[6:8]
    far_bottom, near_bottom = planes[total - 8 : total - 6], planes[total - 6 : total - 4]
    row, col = lax.axis_index("row"), lax.axis_index("col")
    even_row, even_col = row % 2 == 0, col % 2 == 0
    lower_a, lower_b = (row + 1) // 2 % 2 == 0, row % 2 == 1
    row_a, row_b = pairs_a("row"), shifted("row", 1)
    col_a, col_b = pairs_a("col"), shifted("col", 1)

    kept, sent = split(sums, lower_a)
    by_way = lax.axis_size("row") == 4
    far_out = jnp.where(even_row, far_top, far_bottom)
    arrived, extra, near_a, far_a, *far_way = with_edges(
        "row", row_a, sent, early[None],
        jnp.where(even_row, near_bottom, near_top), jnp.where(even_row, far_bottom, far_top),
        *([far_out] if by_way else []),
    )
    kept, early, own_first, *grads = tied(kept + arrived, early + extra[0], own_first, *grads)
    near_out = jnp.where(even_row, near_top, near_bottom)
    if by_way:
        outer = (row == 0) | (row == lax.axis_size("row") - 1)
        edges_out = [jnp.where(outer, far_way[0], near_out)]
    else:
        edges_out = [near_out, far_out]
    kept, sent = split(kept, lower_b)
    arrived, extra, near_b, *far_b = with_edges("row", row_b, sent, early[None], *edges_out)
    above, below = neighbours("row", near_a, near_b)
    tensor = tensor_piece(0, grads)
    kept, early, above, below, tensor = tied(kept + arrived, early + extra[0], above, below, tensor)
    extended, col_first, col_last = call(
        extend_kernel,
        out_shape=(shape32(total, fields, ny), shape32(fields, ny), shape32(fields, ny)),
    )(planes, above, below, own_first, own_last)
    first_edge, last_edge = col_first[None], col_last[None]
    arrived, extra, col_from_a = with_edges("col", col_a, kept, early[None], jnp.where(even_col, last_edge, first_edge))
    tensor = tensor_piece(1, grads, tensor)
    kept, early, tensor = tied(kept + arrived, early + extra[0], tensor)
    arrived, extra, col_from_b = with_edges("col", col_b, kept, early[None], jnp.where(even_col, first_edge, last_edge))
    left, right = (edge[0] for edge in neighbours("col", col_from_a, col_from_b))
    tensor = tensor_piece(2, grads, tensor)
    kept, early, left, right, tensor = tied(kept + arrived, early + extra[0], left, right, tensor)

    later = later_steps("row") + later_steps("col")
    for number, (axis, partner) in enumerate(later):
        arrived, extra = with_edges(axis, partner, kept, early[None])
        kept, early = kept + arrived, early + extra[0]
        if number == 0:
            tensor = call(
                functools.partial(edge_tensor_kernel, scale),
                out_shape=shape32(tiles * count, LANES),
                scratch_shapes=[vmem32(6, fields, ny), vmem32(padded, 5 * ny)],
            )(extended, left, right, col_first, col_last, tensor)
            grad_x, grad_y, ring, shape = call(
                gradient_kernel,
                out_shape=(
                    shape32(total - 4, fields, ny), shape32(total - 4, fields, ny), shape32(5, fields, ny),
                    shape32(2 * nx, count, ny),
                ),
            )(extended, left, right, col_first, col_last)
        kept, early, tensor, shape = tied(kept, early, tensor, shape)
    moments = kept

    kept, sent = split(tensor, lower_a)
    arrived, *far_way = with_edges("row", row_a, sent, *([near_b] if by_way else []))
    far_above, far_below = neighbours("row", far_a, (far_way if by_way else far_b)[0])
    both, mean, pair_cov, offset = call(
        functools.partial(offset_kernel, row_total),
        out_shape=(
            shape32(2, count, count), shape32(count, rows_dev), shape32(1, padded), shape32(count, padded),
        ),
    )(early, first, second, share)
    kept, moments, both, far_above = tied(kept + arrived, moments, both, far_above)
    kept, sent = split(kept, lower_b)
    arrived, other = with_edges("row", row_b, sent, moments[None])
    kept = kept + arrived
    cov_inverse, gram_inverse = call(
        inverse_kernel, out_shape=(shape32(count, count), shape32(count, count))
    )(both)
    moments = joined(moments, other[0], lower_b)
    kept, moments, cov_inverse = tied(kept, moments, cov_inverse)
    sums = joined(moments, swap(moments, "row", row_a), lower_a)
    kept, sums = tied(kept, sums)
    weights, pieces = call(
        functools.partial(weight_kernel, row_total),
        out_shape=(
            jax.ShapeDtypeStruct((2 * count, padded), jnp.bfloat16),
            jax.ShapeDtypeStruct((2 * padded, rows_dev), jnp.bfloat16),
        ),
        scratch_shapes=[vmem32(padded, rows_dev)],
    )(sums, cov_inverse, offset, share, coeffs, mean)
    col_bits = axis_bits("col")
    steps = later_steps("row") + [
        ("col", [i ^ (1 << bit) for i in range(lax.axis_size("col"))]) for bit in col_bits
    ]

    def forcing(start, stop):
        return call(
            functools.partial(forcing_kernel, start),
            out_shape=shape32(2 * (stop - start), count, ny),
            scratch_shapes=[vmem32(padded, 2 * ny)],
        )(weights, extended, grad_x, grad_y)

    def ring_forcing():
        return call(
            ring_forcing_kernel,
            out_shape=(shape32(4, count, ny), shape32(count, ny)),
            scratch_shapes=[vmem32(4, fields, ny), vmem32(padded, 2 * ny)],
        )(weights, extended, far_above, far_below, grad_y, ring)

    works = [functools.partial(forcing, 1 + nx * n // 2, 1 + nx * (n + 1) // 2) for n in range(2)] + [ring_forcing]
    moved = []
    for axis, partner in steps:
        total_kept = kept + swap(kept, axis, partner)
        if works:
            moved.append(works.pop(0)())
        kept, weights, moved = tied(total_kept, weights, moved)
    kept = joined(kept, swap(kept, "row", row_b), lower_b)
    while works:
        moved.append(works.pop(0)())
    moved_rows, moved_ring = moved.pop()
    base = call(smooth_kernel, out_shape=shape32(2 * nx, count, ny))(
        extended, jnp.concatenate([moved_rows[:2], *moved, moved_rows[2:]], axis=0), moved_ring
    )
    kept, base = tied(kept, base)
    tensor = joined(kept, swap(kept, "row", row_a), lower_a)

    new_modes, new_coeffs = call(
        finish_kernel,
        out_shape=(shape32(count * 2 * nx, ny), shape32(count, rows_dev)),
        out_specs=(pl.BlockSpec(memory_space=pltpu.HBM),) * 2,
        scratch_shapes=[vmem32(count * 2 * nx, ny), vmem32(count, rows_dev), pltpu.SemaphoreType.DMA((2,))],
    )(tensor, weights, pieces, gram_inverse, coeffs, mean, pair_cov, share, base, shape)
    return (new_modes.reshape(modes.shape), new_coeffs.T)


def solution(mesh):
    return jax.shard_map(
        on_device,
        mesh=mesh,
        in_specs=(
            P(None, None, "row", "col"),
            P(None, "row", "col"),
            P(("row", "col"), None),
            P(),
            P("row", "col"),
        ),
        out_specs=(P(None, None, "row", "col"), P(("row", "col"), None)),
        check_vma=False,
    )
```

```python
import functools
import math

import jax
import jax.numpy as jnp
import numpy as np
from jax import lax
from jax.experimental import pallas as pl
from jax.experimental.pallas import tpu as pltpu
from jax.sharding import PartitionSpec as P

TIME_STEP = 0.25
VISCOUS = 0.2
PRECISE = lax.Precision.HIGHEST
TILE = 8
LANES = 128
NT = (((1,), (1,)), ((), ()))
NN = (((1,), (0,)), ((), ()))


HALF_TILE = TILE // 2


def pair_start(block):
    return TILE * (TILE * block * (block - 1) // 2 + (HALF_TILE + 1) * block)


def pair_layout(count):
    blocks = count // TILE
    pairs = pair_start(blocks)
    padded = -(-(pairs + count + 2) // LANES) * LANES
    first = np.full((1, padded), -1, np.int32)
    second = np.full((1, padded), -1, np.int32)
    share = np.zeros((1, padded), np.float32)

    def put(row, j, k):
        first[0, row], second[0, row], share[0, row] = j, k, 0.5 if j == k else 1.0

    for block in range(blocks):
        row = pair_start(block)
        base = TILE * block
        for j in range(base):
            for r in range(TILE):
                put(row + TILE * j + r, j, base + r)
        row += TILE * base
        for n in range(HALF_TILE + 1):
            for r in range(TILE):
                if r >= n:
                    put(row + TILE * n + r, base + n, base + r)
                elif n < HALF_TILE:
                    put(row + TILE * n + r, base + TILE - n, base + TILE - n + r)
    share[0, pairs : pairs + count] = 1.0
    return pairs, padded, first, second, share


def pair_tiles(arrays, count):
    blocks = count // TILE
    ids = lax.broadcasted_iota(jnp.int32, (TILE, arrays[0].shape[1]), 0)

    def tile(block):
        return [a[TILE * block : TILE * block + TILE, :] for a in arrays]

    for j in range(count):
        leads = [a[j : j + 1, :] for a in arrays]
        for block in range(j // TILE + 1, blocks):
            yield pair_start(block) + TILE * j, leads, tile(block)
    for block in range(blocks):
        base = TILE * block
        for n in range(HALF_TILE + 1):
            leads, parts = [a[base + n : base + n + 1, :] for a in arrays], tile(block)
            if 0 < n < HALF_TILE:
                other = base + TILE - n
                leads = [jnp.where(ids < n, a[other : other + 1, :], lead) for a, lead in zip(arrays, leads)]
                parts = [jnp.where(ids < n, pltpu.roll(part, n, 0), part) for part in parts]
            yield pair_start(block) + TILE * (base + n), leads, parts


def flow_tiles(arrays, count):
    leads = [a[count : count + 1, :] for a in arrays]
    for block in range(count // TILE):
        rows = slice(TILE * block, TILE * block + TILE)
        yield pair_start(count // TILE) + TILE * block, leads, [a[rows, :] for a in arrays]


def dot32(left, right, dims):
    return lax.dot_general(left, right, dims, precision=PRECISE, preferred_element_type=jnp.float32)


def halves(values):
    high = values.astype(jnp.bfloat16)
    low = (values - high.astype(jnp.float32)).astype(jnp.bfloat16)
    return high, low


def stacked_halves(values):
    high, low = halves(values)
    return jnp.concatenate([high, low], axis=0)


def dot_halves(left_stack, right, dims):
    high, low = halves(right)
    both = lax.dot_general(left_stack, high, dims, preferred_element_type=jnp.float32)
    both += lax.dot_general(left_stack, low, dims, preferred_element_type=jnp.float32)
    rows = left_stack.shape[0] // 2
    return both[:rows] + both[rows:]


def lane_ids(rows):
    return lax.broadcasted_iota(jnp.int32, (rows, LANES), 1)


SECOND = 32
SIDE = 64


def put_lane(packed, ids, plane, lane, target):
    return jnp.where(ids == target, pltpu.roll(plane, (target - lane) % LANES, 1), packed)


def front_kernel(
    scale, modes, flow, water, seeds, strength, amplitudes, planes, sums, early, coeffs, rows
):
    step = coeffs.shape[0]
    total = modes.shape[0] // step
    nx = total // 2
    planes[...] = jnp.zeros(planes.shape, jnp.float32)
    diagonal = lax.broadcasted_iota(jnp.int32, (step, step), 0) == lax.broadcasted_iota(jnp.int32, (step, step), 1)
    heights = jnp.sum(jnp.where(diagonal, amplitudes[...], 0.0), axis=1, keepdims=True)
    wave = jnp.cos(seeds[...].astype(jnp.float32) * (3.0 * math.pi / 8192.0))
    values = strength[...] * heights * (wave + (wave * wave - 0.5))
    coeffs[...] = values
    pairs = pair_start(step // TILE)
    fill_coeff_rows(values, rows)
    rows[pairs + step : pairs + step + 1, :] = jnp.ones((1, values.shape[1]), jnp.float32)
    moments = dot32(values, rows[...], NT)
    tiles = moments.shape[1] // LANES
    for tile in range(tiles):
        sums[tile * step : (tile + 1) * step, :] = moments[:, tile * LANES : (tile + 1) * LANES]
    gram = jnp.zeros((step, step), jnp.float32)
    for x in range(nx):
        mask = water[x : x + 1, :].astype(jnp.float32)
        both = []
        for c in range(2):
            q = 2 * x + c
            field = modes[pl.ds(c * nx + x, step, stride=total), :]
            both.append(field)
            planes[q + 4, 0:step, :] = field
            planes[q + 4, step : step + 1, :] = flow[c * nx + x : c * nx + x + 1, :]
            planes[q + 4, step + 1 : step + 2, :] = mask
        wide = jnp.concatenate(both, axis=1)
        weight = jnp.concatenate([mask, mask], axis=1) * scale
        gram += dot_halves(stacked_halves(wide * weight), wide, NT)
    heads = lax.broadcasted_iota(jnp.int32, (step, step), 0)
    lanes = lax.broadcasted_iota(jnp.int32, (step, step), 1)
    both = jnp.where(lanes < heads, gram, moments[:, pairs : pairs + step])
    corner = jnp.sum(jnp.where(lanes == heads, gram, 0.0), axis=1, keepdims=True)
    rest = jnp.zeros((step, SIDE - step - 2), jnp.float32)
    packed = jnp.concatenate([both, moments[:, pairs + step : pairs + step + 1], corner, rest], axis=1)
    early[...] = jnp.concatenate([packed[: step // 2], packed[step // 2 :]], axis=1)


def fill_coeff_rows(values, rows):
    count = values.shape[0]
    pairs = pair_start(count // TILE)
    for start, (lead,), (part,) in pair_tiles([values], count):
        rows[start : start + TILE, :] = lead * part
    rows[pairs : pairs + count, :] = values
    rows[pairs + count :, :] = jnp.zeros((rows.shape[0] - pairs - count, values.shape[1]), jnp.float32)


def extend_kernel(planes, above, below, first_in, last_in, extended, col_first, col_last):
    total = planes.shape[0]
    fields = planes.shape[1]
    ids = lane_ids(fields)
    extended[...] = planes[...]
    extended[2:4] = above[...]
    extended[total - 4 : total - 2] = below[...]
    first = first_in[...]
    last = last_in[...]
    for c in range(2):
        for plane, lane in ((above[c], c), (below[c], total - 6 + c)):
            first = put_lane(first, ids, plane, 0, lane)
            last = put_lane(last, ids, plane, LANES - 1, lane)
    col_first[...] = first
    col_last[...] = last


def plain_gradient_kernel(planes, grad_x, grad_y, col_first, col_last):
    fields = planes.shape[1]
    ids = lane_ids(fields)
    first = jnp.zeros((fields, LANES), jnp.float32)
    last = jnp.zeros((fields, LANES), jnp.float32)
    for q in range(grad_x.shape[0]):
        grad_x[q] = 0.5 * (planes[q + 6] - planes[q + 2])
        plane = planes[q + 4]
        east = jnp.where(ids == LANES - 1, 0.0, pltpu.roll(plane, LANES - 1, 1))
        west = jnp.where(ids == 0, 0.0, pltpu.roll(plane, 1, 1))
        grad_y[q] = 0.5 * (east - west)
        first = put_lane(first, ids, plane, 0, q + 2)
        first = put_lane(first, ids, plane, 1, q + 2 + SECOND)
        last = put_lane(last, ids, plane, LANES - 1, q + 2)
        last = put_lane(last, ids, plane, LANES - 2, q + 2 + SECOND)
    col_first[...] = first
    col_last[...] = last


def odd_even(packed, ids):
    odd = ids % 2 == 1
    zero = jnp.where(odd, pltpu.roll(packed, 1, 1), packed)
    one = jnp.where(odd, packed, pltpu.roll(packed, LANES - 1, 1))
    return zero, one


def gradient_kernel(extended, left, right, col_first, col_last, grad_x, grad_y, ring, shape):
    fields = extended.shape[1]
    ids = lane_ids(fields)
    from_left = left[...]
    from_right = right[...]
    for q in range(grad_x.shape[0]):
        grad_x[q] = 0.5 * (extended[q + 4] - extended[q])
        plane = extended[q + 2]
        east = put_lane(pltpu.roll(plane, LANES - 1, 1), ids, from_right, q, LANES - 1)
        west = put_lane(pltpu.roll(plane, 1, 1), ids, from_left, q, 0)
        grad_y[q] = 0.5 * (east - west)

    def both(near, far):
        return jnp.where(ids < SIDE, near, pltpu.roll(far, SIDE, 1))

    centre = both(from_left, from_right)
    inner = both(col_first[...], col_last[...])
    outer = pltpu.roll(centre, LANES - SECOND, 1)
    zero, one = odd_even(centre, ids)
    ring[0] = zero
    ring[1] = one
    ring[2] = 0.5 * (pltpu.roll(centre, LANES - 2, 1) - pltpu.roll(centre, 2, 1))
    ring[3] = jnp.where(ids < SIDE, 0.5, -0.5) * (inner - outer)
    ring[4] = centre

    total, count, _ = shape.shape
    beside = centre[0:count, :] * centre[count + 1 : count + 2, :]

    def masked(q):
        return extended[q + 2, 0:count, :] * extended[q + 2, count + 1 : count + 2, :]

    for q in range(total):
        water = extended[q + 4, count + 1 : count + 2, :]
        shape[q] = (TIME_STEP * water) * diffused(masked(q), masked(q + 2), masked(q + 4), beside, q)


def diffused(before, plane, after, beside, q):
    ids = lane_ids(plane.shape[0])
    east = put_lane(pltpu.roll(plane, LANES - 1, 1), ids, beside, q + 2 + SIDE, LANES - 1)
    west = put_lane(pltpu.roll(plane, 1, 1), ids, beside, q + 2, 0)
    return plane + VISCOUS * (before + after + east + west - 4.0 * plane)


def all_tiles(arrays):
    count = arrays[0].shape[0] // TILE * TILE - TILE
    yield from pair_tiles(arrays, count)
    yield from flow_tiles(arrays, count)


def fill_pair_fields(velocity, grads, rows):
    arrays = list(velocity) + [ref for pair in grads for ref in pair]
    for start, leads, parts in all_tiles(arrays):
        for c in range(len(grads)):
            x, y = 2 + 2 * c, 3 + 2 * c
            value = leads[0] * parts[x] + leads[1] * parts[y] + parts[0] * leads[x] + parts[1] * leads[y]
            rows[start : start + TILE, c * LANES : (c + 1) * LANES] = value


def fill_edge_fields(edges, rows):
    for start, leads, parts in all_tiles([ref for edge in edges for ref in edge]):
        for n in range(len(edges)):
            u, d = 2 * n, 2 * n + 1
            value = leads[u] * parts[d] + parts[u] * leads[d]
            rows[start : start + TILE, n * LANES : (n + 1) * LANES] = value


def clear_rest(rows, count):
    used = pair_start(count // TILE) + count
    rows[used:, :] = jnp.zeros((rows.shape[0] - used, rows.shape[1]), jnp.float32)


def add_to_tiles(out, before, stack, rows):
    count = stack.shape[0] // 2
    for first in range(0, rows.shape[0], 2 * LANES):
        last = min(first + 2 * LANES, rows.shape[0])
        value = dot_halves(stack, rows[first:last, :], NT)
        for start in range(first, last, LANES):
            place = slice(start // LANES * count, (start // LANES + 1) * count)
            part = value[:, start - first : start - first + LANES]
            out[place, :] = part if before is None else before[place, :] + part


def tiles_beside(values, count):
    return jnp.concatenate([values[at : at + count, :] for at in range(0, values.shape[0], count)], axis=1)


def tensor_kernel(scale, start, stop, planes, grad_x, grad_y, *refs):
    *before, out, rows = refs
    count = out.shape[0] * LANES // rows.shape[0]
    clear_rest(rows, count)
    out[...] = before[0][...] if before else jnp.zeros(out.shape, jnp.float32)

    def body(x, carry):
        q = 2 * x
        velocity = [planes.at[q + 4], planes.at[q + 5]]
        fill_pair_fields(velocity, [(grad_x.at[q + c], grad_y.at[q + c]) for c in range(2)], rows)
        water = planes[q + 4, count + 1 : count + 2, :] * (-scale)
        weighted = jnp.concatenate([planes[q + 4, 0:count, :] * water, planes[q + 5, 0:count, :] * water], axis=1)
        add_to_tiles(out, out, stacked_halves(weighted), rows)
        return carry

    lax.fori_loop(start, stop, body, 0)


def edge_tensor_kernel(scale, extended, left, right, col_first, col_last, before, out, parts, rows):
    count = out.shape[0] * LANES // rows.shape[0]
    total = extended.shape[0]
    fields = extended.shape[1]
    clear_rest(rows, count)
    ids = lane_ids(fields)
    for c in range(2):
        parts[c] = -0.5 * extended[2 + c]
        parts[2 + c] = 0.5 * extended[total - 4 + c]
    near = (ids >= 2) & (ids < total - 6)
    far = (ids >= 2 + SIDE) & (ids < total - 6 + SIDE)
    parts[4] = jnp.where(near, -0.5 * left[...], jnp.where(far, 0.5 * pltpu.roll(right[...], SIDE, 1), 0.0))
    centre = jnp.where(ids < SIDE, col_first[...], pltpu.roll(col_last[...], SIDE, 1))
    parts[5] = odd_even(centre, ids)[1]
    top, bottom = extended.at[4], extended.at[total - 6]
    fill_edge_fields(
        [
            (top, parts.at[0]), (top, parts.at[1]), (bottom, parts.at[2]), (bottom, parts.at[3]),
            (parts.at[5], parts.at[4]),
        ],
        rows,
    )
    weighted = []
    for plane in (extended[4], extended[5], extended[total - 6], extended[total - 5], centre):
        weighted.append(plane[0:count, :] * (plane[count + 1 : count + 2, :] * (-scale)))
    add_to_tiles(out, before, stacked_halves(jnp.concatenate(weighted, axis=1)), rows)


def inverse_pair(first, second):
    count = first.shape[0]
    row_ids = lax.broadcasted_iota(jnp.int32, (count, count), 0)
    col_ids = lax.broadcasted_iota(jnp.int32, (count, count), 1)
    both = [first, second]
    for k in range(count):
        for n in range(2):
            a = both[n]
            row = a[k : k + 1, :]
            col = a[:, k : k + 1]
            pivot = 1.0 / a[k : k + 1, k : k + 1]
            row = jnp.where(col_ids[0:1] == k, 1.0, row) * pivot
            kept = jnp.where(col_ids == k, 0.0, a)
            both[n] = jnp.where(row_ids == k, row, kept - col * row)
    return both


def offset_kernel(realizations, early, first, second, share, both, mean, pair_cov, offset):
    count, padded = offset.shape
    packed = jnp.concatenate([early[:, 0:SIDE], early[:, SIDE : 2 * SIDE]], axis=0)
    shared = packed[:, 0:count]
    means = packed[:, count : count + 1] * (1.0 / realizations)
    row_ids = lax.broadcasted_iota(jnp.int32, (count, count), 0)
    col_ids = lax.broadcasted_iota(jnp.int32, (count, count), 1)
    turned = shared.T
    raw_second = jnp.where(col_ids >= row_ids, shared, turned) * (1.0 / realizations)
    gram = jnp.where(col_ids < row_ids, shared, turned)
    gram = jnp.where(col_ids == row_ids, packed[:, count + 1 : count + 2], gram)
    mean_row = jnp.sum(jnp.where(row_ids == col_ids, means, 0.0), axis=0, keepdims=True)
    covariance = raw_second - means * mean_row
    both[0] = covariance
    both[1] = gram
    ids = lax.broadcasted_iota(jnp.int32, (count, padded), 0)
    pick_first = (ids == first[...]).astype(jnp.float32)
    pick_second = (ids == second[...]).astype(jnp.float32)
    cov_first = dot32(covariance, pick_first, NN)
    cov_second = dot32(covariance, pick_second, NN)
    mean_first = jnp.sum(pick_first * means, axis=0, keepdims=True)
    mean_second = jnp.sum(pick_second * means, axis=0, keepdims=True)
    cov_pair = jnp.sum(pick_first * cov_second, axis=0, keepdims=True)
    offset[...] = means * (cov_pair + mean_first * mean_second) + mean_first * cov_second + mean_second * cov_first
    mean[...] = jnp.broadcast_to(means, mean.shape)
    pair_cov[...] = cov_pair * share[...]


def inverse_kernel(both, cov_inverse, gram_inverse):
    cov_inverse[...], gram_inverse[...] = inverse_pair(both[0], both[1])


def pair_kernel(coeffs, mean, pieces, rows):
    fill_coeff_rows(coeffs[...] - mean[...], rows)
    pieces[...] = stacked_halves(rows[...])


def weight_kernel(realizations, sums, cov_inverse, offset, share, weights):
    count = cov_inverse.shape[0]
    padded = weights.shape[1]
    pairs = pair_start(count // TILE)
    third = tiles_beside(sums[...], count) * (1.0 / realizations) - offset[...]
    weight_map = dot32(cov_inverse[...], third, NN) * share[...]
    ids = lax.broadcasted_iota(jnp.int32, (count, padded), 0)
    lanes = lax.broadcasted_iota(jnp.int32, (count, padded), 1)
    unit = jnp.where(lanes - pairs == ids, 1.0, 0.0)
    weights[...] = stacked_halves(jnp.where(lanes < pairs, weight_map, unit))


def forcing_kernel(start, weights, extended, grad_x, grad_y, out, rows):
    count = weights.shape[0] // 2
    clear_rest(rows, count)
    stack = weights[...]

    def body(n, carry):
        q = 2 * (start + n)
        velocity = [extended.at[q + 2], extended.at[q + 3]]
        fill_pair_fields(velocity, [(grad_x.at[q + c], grad_y.at[q + c]) for c in range(2)], rows)
        nonlinear = dot_halves(stack, rows[...], NN)
        water = extended[q + 2, count + 1 : count + 2, :]
        for c in range(2):
            part = nonlinear[:, c * LANES : (c + 1) * LANES]
            out[2 * n + c] = water * (extended[q + 2 + c, 0:count, :] - TIME_STEP * part)
        return carry

    lax.fori_loop(0, out.shape[0] // 2, body, 0)


def closing_kernel(weights, extended, far_above, far_below, grad_y, ring, *refs):
    *moved, base, out_rows, edge_x, rows = refs
    count = weights.shape[0] // 2
    total = extended.shape[0]
    clear_rest(rows, count)
    stack = weights[...]
    for c in range(2):
        edge_x[c] = 0.5 * (extended[4 + c] - far_above[c])
        edge_x[2 + c] = 0.5 * (far_below[c] - extended[total - 6 + c])

    def body(n, carry):
        q = n * (total - 6)
        velocity = [extended.at[q + 2], extended.at[q + 3]]
        fill_pair_fields(velocity, [(edge_x.at[2 * n + c], grad_y.at[q + c]) for c in range(2)], rows)
        nonlinear = dot_halves(stack, rows[...], NN)
        water = extended[q + 2, count + 1 : count + 2, :]
        for c in range(2):
            part = nonlinear[:, c * LANES : (c + 1) * LANES]
            out_rows[2 * n + c] = water * (extended[q + 2 + c, 0:count, :] - TIME_STEP * part)
        return carry

    lax.fori_loop(0, 2, body, 0)
    fill_pair_fields([ring.at[0], ring.at[1]], [(ring.at[2], ring.at[3])], rows)
    nonlinear = dot_halves(stack, rows[:, :LANES], NN)
    beside = ring[4, count + 1 : count + 2, :] * (ring[4, 0:count, :] - TIME_STEP * nonlinear)
    planes = [out_rows[0], out_rows[1]]
    for piece in moved:
        planes += [piece[q] for q in range(piece.shape[0])]
    planes += [out_rows[2], out_rows[3]]
    for q in range(base.shape[0]):
        water = extended[q + 4, count + 1 : count + 2, :]
        base[q] = water * diffused(planes[q], planes[q + 2], planes[q + 4], beside, q)


def finish_kernel(
    tensor, weights, pieces, gram_inverse, coeffs, mean, pair_cov, share, base, shape,
    modes_out, coeffs_out, new_modes, new_coeffs, sems,
):
    count = coeffs.shape[0]
    total = base.shape[0]
    inverse = gram_inverse[...]
    tens = tiles_beside(tensor[...], count)
    projected = dot_halves(weights[...], tens, NT)
    stack = stacked_halves(tens * share[...])
    drift = jnp.dot(stack, pieces[0 : tens.shape[1], :], preferred_element_type=jnp.float32)
    drift += jnp.dot(stack, pieces[tens.shape[1] :, :], preferred_element_type=jnp.float32)
    drift = drift[:count] + drift[count:] - jnp.sum(tens * pair_cov[...], axis=1, keepdims=True)
    solved = stacked_halves(dot_halves(stacked_halves(projected), inverse, NN))
    new_coeffs[...] = coeffs[...] - mean[...] + TIME_STEP * dot_halves(stacked_halves(inverse), drift, NN)
    for x in range(total // 2):
        both = jnp.concatenate([shape[2 * x], shape[2 * x + 1]], axis=1)
        change = dot_halves(solved, both, NN)
        for c in range(2):
            value = base[2 * x + c] - change[:, c * LANES : (c + 1) * LANES]
            new_modes[pl.ds(c * (total // 2) + x, count, stride=total), :] = value
    leaving = [
        pltpu.make_async_copy(new_coeffs, coeffs_out, sems.at[0]),
        pltpu.make_async_copy(new_modes, modes_out, sems.at[1]),
    ]
    for leave in leaving:
        leave.start()
    for leave in leaving:
        leave.wait()


def axis_bits(axis):
    count = lax.axis_size(axis)
    assert count & (count - 1) == 0
    return list(range(count.bit_length() - 1))


def swap(values, axis, partner):
    return lax.ppermute(values, axis, list(enumerate(partner)))


def pairs_a(axis):
    return [i ^ 1 for i in range(lax.axis_size(axis))]


def shifted(axis, distance):
    count = lax.axis_size(axis)
    return [(((i - 1) % count ^ distance) + 1) % count for i in range(count)]


def later_steps(axis):
    return [(axis, shifted(axis, 1 << bit)) for bit in axis_bits(axis)[2:]]


def with_edges(axis, partner, values, *edges):
    rows = [values.shape[0]] + [edge.shape[0] * edge.shape[1] for edge in edges]
    flat = [values] + [edge.reshape(-1, edge.shape[-1]) for edge in edges]
    arrived = swap(jnp.concatenate(flat, axis=0), axis, partner)
    ends = np.cumsum(rows)
    return [arrived[: rows[0]]] + [
        arrived[ends[n] : ends[n + 1]].reshape(edge.shape) for n, edge in enumerate(edges)
    ]


def neighbours(axis, from_a, from_b):
    here = lax.axis_index(axis)
    even = here % 2 == 0
    before = jnp.where(here == 0, 0.0, jnp.where(even, from_b, from_a))
    after = jnp.where(here == lax.axis_size(axis) - 1, 0.0, jnp.where(even, from_a, from_b))
    return before, after


def split(values, lower):
    half = values.shape[0] // 2
    top, bottom = values[:half], values[half:]
    return jnp.where(lower, top, bottom), jnp.where(lower, bottom, top)


def joined(kept, other, lower):
    return jnp.concatenate([jnp.where(lower, kept, other), jnp.where(lower, other, kept)], axis=0)


def tied(*values):
    return lax.optimization_barrier(values)


def shape32(*dims):
    return jax.ShapeDtypeStruct(dims, jnp.float32)


def work(amount):
    return pl.CostEstimate(flops=amount * 10**9, bytes_accessed=2**20, transcendentals=0)


def vmem32(*dims):
    return pltpu.VMEM(dims, jnp.float32)


PARAMS = pltpu.CompilerParams(vmem_limit_bytes=32 * 1024 * 1024)


def on_device(modes, mean_flow, seeds, amplitudes, water_mask):
    count, _, nx, ny = modes.shape
    devices = lax.axis_size("row") * lax.axis_size("col")
    rows_dev = seeds.shape[0]
    row_total = rows_dev * devices
    scale = 1.0 / (2.0 * nx * ny * devices)
    pairs, padded, first, second, share = pair_layout(count)
    tiles = padded // LANES
    fields = count + TILE
    total = 2 * (nx + 4)
    assert ny == LANES and 2 * (nx + 2) <= SECOND and count % (2 * TILE) == 0
    call = functools.partial(pl.pallas_call, compiler_params=PARAMS)
    assert min(lax.axis_size("row"), lax.axis_size("col")) >= 4

    first_row = lax.axis_index(("row", "col")) * rows_dev
    row_ids = (first_row + jnp.arange(rows_dev, dtype=jnp.int32)).astype(jnp.float32)
    strength = (0.5 + row_ids / row_total).reshape(1, rows_dev)
    planes, sums, early, coeffs = call(
        functools.partial(front_kernel, scale),
        out_shape=(
            shape32(total, fields, ny), shape32(tiles * count, LANES), shape32(count // 2, LANES),
            shape32(count, rows_dev),
        ),
        scratch_shapes=[vmem32(padded, rows_dev)],
    )(
        modes.reshape(count * 2 * nx, ny), mean_flow.reshape(2 * nx, ny), water_mask, seeds.T,
        strength, amplitudes.reshape(1, count),
    )

    *grads, own_first, own_last = call(
        plain_gradient_kernel,
        out_shape=(
            shape32(2 * nx, fields, ny), shape32(2 * nx, fields, ny), shape32(fields, ny), shape32(fields, ny),
        ),
    )(planes)

    def tensor_piece(number, grads, *before):
        start, stop = nx * number // 3, nx * (number + 1) // 3
        return call(
            functools.partial(tensor_kernel, scale, start, stop),
            out_shape=shape32(tiles * count, LANES),
            scratch_shapes=[vmem32(padded, 2 * ny)],
        )(planes, *grads, *before)

    near_top, far_top = planes[4:6], planes[6:8]
    far_bottom, near_bottom = planes[total - 8 : total - 6], planes[total - 6 : total - 4]
    row, col = lax.axis_index("row"), lax.axis_index("col")
    even_row, even_col = row % 2 == 0, col % 2 == 0
    lower_a, lower_b = (row + 1) // 2 % 2 == 0, row % 2 == 1
    row_a, row_b = pairs_a("row"), shifted("row", 1)
    col_a, col_b = pairs_a("col"), shifted("col", 1)

    kept, sent = split(sums, lower_a)
    by_way = lax.axis_size("row") == 4
    far_out = jnp.where(even_row, far_top, far_bottom)
    arrived, extra, near_a, far_a, *far_way = with_edges(
        "row", row_a, sent, early[None],
        jnp.where(even_row, near_bottom, near_top), jnp.where(even_row, far_bottom, far_top),
        *([far_out] if by_way else []),
    )
    kept, early, own_first, *grads = tied(kept + arrived, early + extra[0], own_first, *grads)
    near_out = jnp.where(even_row, near_top, near_bottom)
    if by_way:
        outer = (row == 0) | (row == lax.axis_size("row") - 1)
        edges_out = [jnp.where(outer, far_way[0], near_out)]
    else:
        edges_out = [near_out, far_out]
    kept, sent = split(kept, lower_b)
    arrived, extra, near_b, *far_b = with_edges("row", row_b, sent, early[None], *edges_out)
    above, below = neighbours("row", near_a, near_b)
    tensor = tensor_piece(0, grads)
    kept, early, above, below, tensor = tied(kept + arrived, early + extra[0], above, below, tensor)
    extended, col_first, col_last = call(
        extend_kernel,
        out_shape=(shape32(total, fields, ny), shape32(fields, ny), shape32(fields, ny)),
    )(planes, above, below, own_first, own_last)
    first_edge, last_edge = col_first[None], col_last[None]
    arrived, extra, col_from_a = with_edges("col", col_a, kept, early[None], jnp.where(even_col, last_edge, first_edge))
    tensor = tensor_piece(1, grads, tensor)
    kept, early, tensor = tied(kept + arrived, early + extra[0], tensor)
    arrived, extra, col_from_b = with_edges("col", col_b, kept, early[None], jnp.where(even_col, first_edge, last_edge))
    left, right = (edge[0] for edge in neighbours("col", col_from_a, col_from_b))
    tensor = tensor_piece(2, grads, tensor)
    kept, early, left, right, tensor = tied(kept + arrived, early + extra[0], left, right, tensor)

    later = later_steps("row") + later_steps("col")
    for number, (axis, partner) in enumerate(later):
        arrived, extra = with_edges(axis, partner, kept, early[None])
        kept, early = kept + arrived, early + extra[0]
        if number == 0:
            tensor = call(
                functools.partial(edge_tensor_kernel, scale),
                out_shape=shape32(tiles * count, LANES),
                scratch_shapes=[vmem32(6, fields, ny), vmem32(padded, 5 * ny)],
            )(extended, left, right, col_first, col_last, tensor)
            grad_x, grad_y, ring, shape = call(
                gradient_kernel,
                out_shape=(
                    shape32(total - 4, fields, ny), shape32(total - 4, fields, ny), shape32(5, fields, ny),
                    shape32(2 * nx, count, ny),
                ),
            )(extended, left, right, col_first, col_last)
        kept, early, tensor, shape = tied(kept, early, tensor, shape)
    moments = kept

    kept, sent = split(tensor, lower_a)
    arrived, *far_way = with_edges("row", row_a, sent, *([near_b] if by_way else []))
    far_above, far_below = neighbours("row", far_a, (far_way if by_way else far_b)[0])
    both, mean, pair_cov, offset = call(
        functools.partial(offset_kernel, row_total),
        out_shape=(
            shape32(2, count, count), shape32(count, rows_dev), shape32(1, padded), shape32(count, padded),
        ),
    )(early, first, second, share)
    kept, moments, both, far_above = tied(kept + arrived, moments, both, far_above)
    kept, sent = split(kept, lower_b)
    arrived, other = with_edges("row", row_b, sent, moments[None])
    kept = kept + arrived
    cov_inverse, gram_inverse = call(
        inverse_kernel, out_shape=(shape32(count, count), shape32(count, count))
    )(both)
    moments = joined(moments, other[0], lower_b)
    kept, moments, cov_inverse = tied(kept, moments, cov_inverse)
    moments, late_coeffs = tied(moments, coeffs)
    pieces = call(
        pair_kernel,
        out_shape=jax.ShapeDtypeStruct((2 * padded, rows_dev), jnp.bfloat16),
        scratch_shapes=[vmem32(padded, rows_dev)],
    )(late_coeffs, mean)
    sums = joined(moments, swap(moments, "row", row_a), lower_a)
    kept, pieces = tied(kept, pieces)
    col_bits = axis_bits("col")
    steps = later_steps("row") + [
        ("col", [i ^ (1 << bit) for i in range(lax.axis_size("col"))]) for bit in col_bits
    ]

    def forcing(weights, start, stop):
        return call(
            functools.partial(forcing_kernel, start),
            cost_estimate=work(3),
            out_shape=shape32(2 * (stop - start), count, ny),
            scratch_shapes=[vmem32(padded, 2 * ny)],
        )(weights, extended, grad_x, grad_y)

    weights = None
    moved = []
    for number, (axis, partner) in enumerate(steps):
        total_kept = kept + swap(kept, axis, partner)
        if number == 0:
            kept, sums = tied(total_kept, sums)
            continue
        if weights is None:
            weights = call(
                functools.partial(weight_kernel, row_total),
                cost_estimate=work(1),
                out_shape=jax.ShapeDtypeStruct((2 * count, padded), jnp.bfloat16),
            )(sums, cov_inverse, offset, share)
        if number < 3:
            moved.append(forcing(weights, 1 + nx * (number - 1) // 2, 1 + nx * number // 2))
        kept, weights, moved = tied(total_kept, weights, moved)
    kept = joined(kept, swap(kept, "row", row_b), lower_b)
    base = call(
        closing_kernel,
        out_shape=shape32(2 * nx, count, ny),
        scratch_shapes=[vmem32(4, count, ny), vmem32(4, fields, ny), vmem32(padded, 2 * ny)],
    )(weights, extended, far_above, far_below, grad_y, ring, *moved)
    kept, base = tied(kept, base)
    tensor = joined(kept, swap(kept, "row", row_a), lower_a)

    new_modes, new_coeffs = call(
        finish_kernel,
        out_shape=(shape32(count * 2 * nx, ny), shape32(count, rows_dev)),
        out_specs=(pl.BlockSpec(memory_space=pltpu.HBM),) * 2,
        scratch_shapes=[vmem32(count * 2 * nx, ny), vmem32(count, rows_dev), pltpu.SemaphoreType.DMA((2,))],
    )(tensor, weights, pieces, gram_inverse, coeffs, mean, pair_cov, share, base, shape)
    return (new_modes.reshape(modes.shape), new_coeffs.T)


def solution(mesh):
    return jax.shard_map(
        on_device,
        mesh=mesh,
        in_specs=(
            P(None, None, "row", "col"),
            P(None, "row", "col"),
            P(("row", "col"), None),
            P(),
            P("row", "col"),
        ),
        out_specs=(P(None, None, "row", "col"), P(("row", "col"), None)),
        check_vma=False,
    )
```

```python
import functools
import math

import jax
import jax.numpy as jnp
import numpy as np
from jax import lax
from jax.experimental import pallas as pl
from jax.experimental.pallas import tpu as pltpu
from jax.sharding import PartitionSpec as P

TIME_STEP = 0.25
VISCOUS = 0.2
PRECISE = lax.Precision.HIGHEST
TILE = 8
LANES = 128
NT = (((1,), (1,)), ((), ()))
NN = (((1,), (0,)), ((), ()))


HALF_TILE = TILE // 2


def pair_start(block):
    return TILE * (TILE * block * (block - 1) // 2 + (HALF_TILE + 1) * block)


def pair_layout(count):
    blocks = count // TILE
    pairs = pair_start(blocks)
    padded = -(-(pairs + count + 2) // LANES) * LANES
    first = np.full((1, padded), -1, np.int32)
    second = np.full((1, padded), -1, np.int32)
    share = np.zeros((1, padded), np.float32)

    def put(row, j, k):
        first[0, row], second[0, row], share[0, row] = j, k, 0.5 if j == k else 1.0

    for block in range(blocks):
        row = pair_start(block)
        base = TILE * block
        for j in range(base):
            for r in range(TILE):
                put(row + TILE * j + r, j, base + r)
        row += TILE * base
        for n in range(HALF_TILE + 1):
            for r in range(TILE):
                if r >= n:
                    put(row + TILE * n + r, base + n, base + r)
                elif n < HALF_TILE:
                    put(row + TILE * n + r, base + TILE - n, base + TILE - n + r)
    share[0, pairs : pairs + count] = 1.0
    return pairs, padded, first, second, share


def pair_tiles(arrays, count):
    blocks = count // TILE
    ids = lax.broadcasted_iota(jnp.int32, (TILE, arrays[0].shape[1]), 0)

    def tile(block):
        return [a[TILE * block : TILE * block + TILE, :] for a in arrays]

    for j in range(count):
        leads = [a[j : j + 1, :] for a in arrays]
        for block in range(j // TILE + 1, blocks):
            yield pair_start(block) + TILE * j, leads, tile(block)
    for block in range(blocks):
        base = TILE * block
        for n in range(HALF_TILE + 1):
            leads, parts = [a[base + n : base + n + 1, :] for a in arrays], tile(block)
            if 0 < n < HALF_TILE:
                other = base + TILE - n
                leads = [jnp.where(ids < n, a[other : other + 1, :], lead) for a, lead in zip(arrays, leads)]
                parts = [jnp.where(ids < n, pltpu.roll(part, n, 0), part) for part in parts]
            yield pair_start(block) + TILE * (base + n), leads, parts


def flow_tiles(arrays, count):
    leads = [a[count : count + 1, :] for a in arrays]
    for block in range(count // TILE):
        rows = slice(TILE * block, TILE * block + TILE)
        yield pair_start(count // TILE) + TILE * block, leads, [a[rows, :] for a in arrays]


def dot32(left, right, dims):
    return lax.dot_general(left, right, dims, precision=PRECISE, preferred_element_type=jnp.float32)


def halves(values):
    high = values.astype(jnp.bfloat16)
    low = (values - high.astype(jnp.float32)).astype(jnp.bfloat16)
    return high, low


def stacked_halves(values):
    high, low = halves(values)
    return jnp.concatenate([high, low], axis=0)


def dot_halves(left_stack, right, dims):
    high, low = halves(right)
    both = lax.dot_general(left_stack, high, dims, preferred_element_type=jnp.float32)
    both += lax.dot_general(left_stack, low, dims, preferred_element_type=jnp.float32)
    rows = left_stack.shape[0] // 2
    return both[:rows] + both[rows:]


def lane_ids(rows):
    return lax.broadcasted_iota(jnp.int32, (rows, LANES), 1)


SECOND = 32
SIDE = 64


def put_lane(packed, ids, plane, lane, target):
    return jnp.where(ids == target, pltpu.roll(plane, (target - lane) % LANES, 1), packed)


def front_kernel(
    scale, modes, flow, water, seeds, strength, amplitudes, planes, sums, early, coeffs, rows
):
    step = coeffs.shape[0]
    total = modes.shape[0] // step
    nx = total // 2
    planes[...] = jnp.zeros(planes.shape, jnp.float32)
    diagonal = lax.broadcasted_iota(jnp.int32, (step, step), 0) == lax.broadcasted_iota(jnp.int32, (step, step), 1)
    heights = jnp.sum(jnp.where(diagonal, amplitudes[...], 0.0), axis=1, keepdims=True)
    wave = jnp.cos(seeds[...].astype(jnp.float32) * (3.0 * math.pi / 8192.0))
    values = strength[...] * heights * (wave + (wave * wave - 0.5))
    coeffs[...] = values
    pairs = pair_start(step // TILE)
    fill_coeff_rows(values, rows)
    rows[pairs + step : pairs + step + 1, :] = jnp.ones((1, values.shape[1]), jnp.float32)
    moments = dot32(values, rows[...], NT)
    tiles = moments.shape[1] // LANES
    for tile in range(tiles):
        sums[tile * step : (tile + 1) * step, :] = moments[:, tile * LANES : (tile + 1) * LANES]
    gram = jnp.zeros((step, step), jnp.float32)
    for x in range(nx):
        mask = water[x : x + 1, :].astype(jnp.float32)
        both = []
        for c in range(2):
            q = 2 * x + c
            field = modes[pl.ds(c * nx + x, step, stride=total), :]
            both.append(field)
            planes[q + 4, 0:step, :] = field
            planes[q + 4, step : step + 1, :] = flow[c * nx + x : c * nx + x + 1, :]
            planes[q + 4, step + 1 : step + 2, :] = mask
        wide = jnp.concatenate(both, axis=1)
        weight = jnp.concatenate([mask, mask], axis=1) * scale
        gram += dot_halves(stacked_halves(wide * weight), wide, NT)
    heads = lax.broadcasted_iota(jnp.int32, (step, step), 0)
    lanes = lax.broadcasted_iota(jnp.int32, (step, step), 1)
    both = jnp.where(lanes < heads, gram, moments[:, pairs : pairs + step])
    corner = jnp.sum(jnp.where(lanes == heads, gram, 0.0), axis=1, keepdims=True)
    rest = jnp.zeros((step, SIDE - step - 2), jnp.float32)
    packed = jnp.concatenate([both, moments[:, pairs + step : pairs + step + 1], corner, rest], axis=1)
    early[...] = jnp.concatenate([packed[: step // 2], packed[step // 2 :]], axis=1)


def fill_coeff_rows(values, rows):
    count = values.shape[0]
    pairs = pair_start(count // TILE)
    for start, (lead,), (part,) in pair_tiles([values], count):
        rows[start : start + TILE, :] = lead * part
    rows[pairs : pairs + count, :] = values
    rows[pairs + count :, :] = jnp.zeros((rows.shape[0] - pairs - count, values.shape[1]), jnp.float32)


def extend_kernel(planes, above, below, first_in, last_in, extended, col_first, col_last):
    total = planes.shape[0]
    fields = planes.shape[1]
    ids = lane_ids(fields)
    extended[...] = planes[...]
    extended[2:4] = above[...]
    extended[total - 4 : total - 2] = below[...]
    first = first_in[...]
    last = last_in[...]
    for c in range(2):
        for plane, lane in ((above[c], c), (below[c], total - 6 + c)):
            first = put_lane(first, ids, plane, 0, lane)
            last = put_lane(last, ids, plane, LANES - 1, lane)
    col_first[...] = first
    col_last[...] = last


def plain_gradient_kernel(planes, grad_x, grad_y, col_first, col_last):
    fields = planes.shape[1]
    ids = lane_ids(fields)
    first = jnp.zeros((fields, LANES), jnp.float32)
    last = jnp.zeros((fields, LANES), jnp.float32)
    for q in range(grad_x.shape[0]):
        grad_x[q] = 0.5 * (planes[q + 6] - planes[q + 2])
        plane = planes[q + 4]
        east = jnp.where(ids == LANES - 1, 0.0, pltpu.roll(plane, LANES - 1, 1))
        west = jnp.where(ids == 0, 0.0, pltpu.roll(plane, 1, 1))
        grad_y[q] = 0.5 * (east - west)
        first = put_lane(first, ids, plane, 0, q + 2)
        first = put_lane(first, ids, plane, 1, q + 2 + SECOND)
        last = put_lane(last, ids, plane, LANES - 1, q + 2)
        last = put_lane(last, ids, plane, LANES - 2, q + 2 + SECOND)
    col_first[...] = first
    col_last[...] = last


def odd_even(packed, ids):
    odd = ids % 2 == 1
    zero = jnp.where(odd, pltpu.roll(packed, 1, 1), packed)
    one = jnp.where(odd, packed, pltpu.roll(packed, LANES - 1, 1))
    return zero, one


def gradient_kernel(extended, left, right, col_first, col_last, grad_x, grad_y, ring, shape):
    fields = extended.shape[1]
    ids = lane_ids(fields)
    from_left = left[...]
    from_right = right[...]
    for q in range(grad_x.shape[0]):
        grad_x[q] = 0.5 * (extended[q + 4] - extended[q])
        plane = extended[q + 2]
        east = put_lane(pltpu.roll(plane, LANES - 1, 1), ids, from_right, q, LANES - 1)
        west = put_lane(pltpu.roll(plane, 1, 1), ids, from_left, q, 0)
        grad_y[q] = 0.5 * (east - west)

    def both(near, far):
        return jnp.where(ids < SIDE, near, pltpu.roll(far, SIDE, 1))

    centre = both(from_left, from_right)
    inner = both(col_first[...], col_last[...])
    outer = pltpu.roll(centre, LANES - SECOND, 1)
    zero, one = odd_even(centre, ids)
    ring[0] = zero
    ring[1] = one
    ring[2] = 0.5 * (pltpu.roll(centre, LANES - 2, 1) - pltpu.roll(centre, 2, 1))
    ring[3] = jnp.where(ids < SIDE, 0.5, -0.5) * (inner - outer)
    ring[4] = centre

    total, count, _ = shape.shape
    beside = centre[0:count, :] * centre[count + 1 : count + 2, :]

    def masked(q):
        return extended[q + 2, 0:count, :] * extended[q + 2, count + 1 : count + 2, :]

    for q in range(total):
        water = extended[q + 4, count + 1 : count + 2, :]
        shape[q] = (TIME_STEP * water) * diffused(masked(q), masked(q + 2), masked(q + 4), beside, q)


def diffused(before, plane, after, beside, q):
    ids = lane_ids(plane.shape[0])
    east = put_lane(pltpu.roll(plane, LANES - 1, 1), ids, beside, q + 2 + SIDE, LANES - 1)
    west = put_lane(pltpu.roll(plane, 1, 1), ids, beside, q + 2, 0)
    return plane + VISCOUS * (before + after + east + west - 4.0 * plane)


def all_tiles(arrays):
    count = arrays[0].shape[0] // TILE * TILE - TILE
    yield from pair_tiles(arrays, count)
    yield from flow_tiles(arrays, count)


def fill_pair_fields(velocity, grads, rows):
    arrays = list(velocity) + [ref for pair in grads for ref in pair]
    for start, leads, parts in all_tiles(arrays):
        for c in range(len(grads)):
            x, y = 2 + 2 * c, 3 + 2 * c
            value = leads[0] * parts[x] + leads[1] * parts[y] + parts[0] * leads[x] + parts[1] * leads[y]
            rows[start : start + TILE, c * LANES : (c + 1) * LANES] = value


def fill_edge_fields(edges, rows):
    for start, leads, parts in all_tiles([ref for edge in edges for ref in edge]):
        for n in range(len(edges)):
            u, d = 2 * n, 2 * n + 1
            value = leads[u] * parts[d] + parts[u] * leads[d]
            rows[start : start + TILE, n * LANES : (n + 1) * LANES] = value


def clear_rest(rows, count):
    used = pair_start(count // TILE) + count
    rows[used:, :] = jnp.zeros((rows.shape[0] - used, rows.shape[1]), jnp.float32)


def add_to_tiles(out, before, stack, rows):
    count = stack.shape[0] // 2
    for first in range(0, rows.shape[0], 2 * LANES):
        last = min(first + 2 * LANES, rows.shape[0])
        value = dot_halves(stack, rows[first:last, :], NT)
        for start in range(first, last, LANES):
            place = slice(start // LANES * count, (start // LANES + 1) * count)
            part = value[:, start - first : start - first + LANES]
            out[place, :] = part if before is None else before[place, :] + part


def tiles_beside(values, count):
    return jnp.concatenate([values[at : at + count, :] for at in range(0, values.shape[0], count)], axis=1)


def tensor_kernel(scale, start, stop, planes, grad_x, grad_y, *refs):
    *before, out, rows = refs
    count = out.shape[0] * LANES // rows.shape[0]
    clear_rest(rows, count)
    out[...] = before[0][...] if before else jnp.zeros(out.shape, jnp.float32)

    def body(x, carry):
        q = 2 * x
        velocity = [planes.at[q + 4], planes.at[q + 5]]
        fill_pair_fields(velocity, [(grad_x.at[q + c], grad_y.at[q + c]) for c in range(2)], rows)
        water = planes[q + 4, count + 1 : count + 2, :] * (-scale)
        weighted = jnp.concatenate([planes[q + 4, 0:count, :] * water, planes[q + 5, 0:count, :] * water], axis=1)
        add_to_tiles(out, out, stacked_halves(weighted), rows)
        return carry

    lax.fori_loop(start, stop, body, 0)


def edge_tensor_kernel(scale, extended, left, right, col_first, col_last, before, out, parts, rows):
    count = out.shape[0] * LANES // rows.shape[0]
    total = extended.shape[0]
    fields = extended.shape[1]
    clear_rest(rows, count)
    ids = lane_ids(fields)
    for c in range(2):
        parts[c] = -0.5 * extended[2 + c]
        parts[2 + c] = 0.5 * extended[total - 4 + c]
    near = (ids >= 2) & (ids < total - 6)
    far = (ids >= 2 + SIDE) & (ids < total - 6 + SIDE)
    parts[4] = jnp.where(near, -0.5 * left[...], jnp.where(far, 0.5 * pltpu.roll(right[...], SIDE, 1), 0.0))
    centre = jnp.where(ids < SIDE, col_first[...], pltpu.roll(col_last[...], SIDE, 1))
    parts[5] = odd_even(centre, ids)[1]
    top, bottom = extended.at[4], extended.at[total - 6]
    fill_edge_fields(
        [
            (top, parts.at[0]), (top, parts.at[1]), (bottom, parts.at[2]), (bottom, parts.at[3]),
            (parts.at[5], parts.at[4]),
        ],
        rows,
    )
    weighted = []
    for plane in (extended[4], extended[5], extended[total - 6], extended[total - 5], centre):
        weighted.append(plane[0:count, :] * (plane[count + 1 : count + 2, :] * (-scale)))
    add_to_tiles(out, before, stacked_halves(jnp.concatenate(weighted, axis=1)), rows)


def inverse_pair(first, second):
    count = first.shape[0]
    row_ids = lax.broadcasted_iota(jnp.int32, (count, count), 0)
    col_ids = lax.broadcasted_iota(jnp.int32, (count, count), 1)
    both = [first, second]
    for k in range(count):
        for n in range(2):
            a = both[n]
            row = a[k : k + 1, :]
            col = a[:, k : k + 1]
            pivot = 1.0 / a[k : k + 1, k : k + 1]
            row = jnp.where(col_ids[0:1] == k, 1.0, row) * pivot
            kept = jnp.where(col_ids == k, 0.0, a)
            both[n] = jnp.where(row_ids == k, row, kept - col * row)
    return both


def offset_kernel(realizations, early, first, second, share, both, mean, pair_cov, offset):
    count, padded = offset.shape
    packed = jnp.concatenate([early[:, 0:SIDE], early[:, SIDE : 2 * SIDE]], axis=0)
    shared = packed[:, 0:count]
    means = packed[:, count : count + 1] * (1.0 / realizations)
    row_ids = lax.broadcasted_iota(jnp.int32, (count, count), 0)
    col_ids = lax.broadcasted_iota(jnp.int32, (count, count), 1)
    turned = shared.T
    raw_second = jnp.where(col_ids >= row_ids, shared, turned) * (1.0 / realizations)
    gram = jnp.where(col_ids < row_ids, shared, turned)
    gram = jnp.where(col_ids == row_ids, packed[:, count + 1 : count + 2], gram)
    mean_row = jnp.sum(jnp.where(row_ids == col_ids, means, 0.0), axis=0, keepdims=True)
    covariance = raw_second - means * mean_row
    both[0] = covariance
    both[1] = gram
    ids = lax.broadcasted_iota(jnp.int32, (count, padded), 0)
    pick_first = (ids == first[...]).astype(jnp.float32)
    pick_second = (ids == second[...]).astype(jnp.float32)
    cov_first = dot32(covariance, pick_first, NN)
    cov_second = dot32(covariance, pick_second, NN)
    mean_first = jnp.sum(pick_first * means, axis=0, keepdims=True)
    mean_second = jnp.sum(pick_second * means, axis=0, keepdims=True)
    cov_pair = jnp.sum(pick_first * cov_second, axis=0, keepdims=True)
    offset[...] = means * (cov_pair + mean_first * mean_second) + mean_first * cov_second + mean_second * cov_first
    mean[...] = jnp.broadcast_to(means, mean.shape)
    pair_cov[...] = cov_pair * share[...]


def inverse_kernel(both, cov_inverse, gram_inverse):
    cov_inverse[...], gram_inverse[...] = inverse_pair(both[0], both[1])


def pair_kernel(coeffs, mean, pieces, rows):
    fill_coeff_rows(coeffs[...] - mean[...], rows)
    pieces[...] = stacked_halves(rows[...])


def weight_kernel(realizations, sums, cov_inverse, offset, share, weights):
    count = cov_inverse.shape[0]
    padded = weights.shape[1]
    pairs = pair_start(count // TILE)
    third = tiles_beside(sums[...], count) * (1.0 / realizations) - offset[...]
    weight_map = dot32(cov_inverse[...], third, NN) * share[...]
    ids = lax.broadcasted_iota(jnp.int32, (count, padded), 0)
    lanes = lax.broadcasted_iota(jnp.int32, (count, padded), 1)
    unit = jnp.where(lanes - pairs == ids, 1.0, 0.0)
    weights[...] = stacked_halves(jnp.where(lanes < pairs, weight_map, unit))


def forcing_kernel(start, weights, extended, grad_x, grad_y, out, rows):
    count = weights.shape[0] // 2
    clear_rest(rows, count)
    stack = weights[...]

    def body(n, carry):
        q = 2 * (start + n)
        velocity = [extended.at[q + 2], extended.at[q + 3]]
        fill_pair_fields(velocity, [(grad_x.at[q + c], grad_y.at[q + c]) for c in range(2)], rows)
        nonlinear = dot_halves(stack, rows[...], NN)
        water = extended[q + 2, count + 1 : count + 2, :]
        for c in range(2):
            part = nonlinear[:, c * LANES : (c + 1) * LANES]
            out[2 * n + c] = water * (extended[q + 2 + c, 0:count, :] - TIME_STEP * part)
        return carry

    lax.fori_loop(0, out.shape[0] // 2, body, 0)


def closing_kernel(weights, extended, far_above, far_below, grad_y, ring, *refs):
    *moved, base, out_rows, edge_x, rows = refs
    count = weights.shape[0] // 2
    total = extended.shape[0]
    clear_rest(rows, count)
    stack = weights[...]
    for c in range(2):
        edge_x[c] = 0.5 * (extended[4 + c] - far_above[c])
        edge_x[2 + c] = 0.5 * (far_below[c] - extended[total - 6 + c])

    def body(n, carry):
        q = n * (total - 6)
        velocity = [extended.at[q + 2], extended.at[q + 3]]
        fill_pair_fields(velocity, [(edge_x.at[2 * n + c], grad_y.at[q + c]) for c in range(2)], rows)
        nonlinear = dot_halves(stack, rows[...], NN)
        water = extended[q + 2, count + 1 : count + 2, :]
        for c in range(2):
            part = nonlinear[:, c * LANES : (c + 1) * LANES]
            out_rows[2 * n + c] = water * (extended[q + 2 + c, 0:count, :] - TIME_STEP * part)
        return carry

    lax.fori_loop(0, 2, body, 0)
    fill_pair_fields([ring.at[0], ring.at[1]], [(ring.at[2], ring.at[3])], rows)
    nonlinear = dot_halves(stack, rows[:, :LANES], NN)
    beside = ring[4, count + 1 : count + 2, :] * (ring[4, 0:count, :] - TIME_STEP * nonlinear)
    planes = [out_rows[0], out_rows[1]]
    for piece in moved:
        planes += [piece[q] for q in range(piece.shape[0])]
    planes += [out_rows[2], out_rows[3]]
    for q in range(base.shape[0]):
        water = extended[q + 4, count + 1 : count + 2, :]
        base[q] = water * diffused(planes[q], planes[q + 2], planes[q + 4], beside, q)


def finish_kernel(
    tensor, weights, pieces, gram_inverse, coeffs, mean, pair_cov, share, base, shape,
    modes_out, coeffs_out, new_modes, new_coeffs, sems,
):
    count = coeffs.shape[0]
    total = base.shape[0]
    inverse = gram_inverse[...]
    tens = tiles_beside(tensor[...], count)
    projected = dot_halves(weights[...], tens, NT)
    stack = stacked_halves(tens * share[...])
    drift = jnp.dot(stack, pieces[0 : tens.shape[1], :], preferred_element_type=jnp.float32)
    drift += jnp.dot(stack, pieces[tens.shape[1] :, :], preferred_element_type=jnp.float32)
    drift = drift[:count] + drift[count:] - jnp.sum(tens * pair_cov[...], axis=1, keepdims=True)
    solved = stacked_halves(dot_halves(stacked_halves(projected), inverse, NN))
    new_coeffs[...] = coeffs[...] - mean[...] + TIME_STEP * dot_halves(stacked_halves(inverse), drift, NN)
    for x in range(total // 2):
        both = jnp.concatenate([shape[2 * x], shape[2 * x + 1]], axis=1)
        change = dot_halves(solved, both, NN)
        for c in range(2):
            value = base[2 * x + c] - change[:, c * LANES : (c + 1) * LANES]
            new_modes[pl.ds(c * (total // 2) + x, count, stride=total), :] = value
    leaving = [
        pltpu.make_async_copy(new_coeffs, coeffs_out, sems.at[0]),
        pltpu.make_async_copy(new_modes, modes_out, sems.at[1]),
    ]
    for leave in leaving:
        leave.start()
    for leave in leaving:
        leave.wait()


def axis_bits(axis):
    count = lax.axis_size(axis)
    assert count & (count - 1) == 0
    return list(range(count.bit_length() - 1))


def swap(values, axis, partner):
    return lax.ppermute(values, axis, list(enumerate(partner)))


def pairs_a(axis):
    return [i ^ 1 for i in range(lax.axis_size(axis))]


def shifted(axis, distance):
    count = lax.axis_size(axis)
    return [(((i - 1) % count ^ distance) + 1) % count for i in range(count)]


def later_steps(axis):
    return [(axis, shifted(axis, 1 << bit)) for bit in axis_bits(axis)[2:]]


def with_edges(axis, partner, values, *edges):
    rows = [values.shape[0]] + [edge.shape[0] * edge.shape[1] for edge in edges]
    flat = [values] + [edge.reshape(-1, edge.shape[-1]) for edge in edges]
    arrived = swap(jnp.concatenate(flat, axis=0), axis, partner)
    ends = np.cumsum(rows)
    return [arrived[: rows[0]]] + [
        arrived[ends[n] : ends[n + 1]].reshape(edge.shape) for n, edge in enumerate(edges)
    ]


def neighbours(axis, from_a, from_b):
    here = lax.axis_index(axis)
    even = here % 2 == 0
    before = jnp.where(here == 0, 0.0, jnp.where(even, from_b, from_a))
    after = jnp.where(here == lax.axis_size(axis) - 1, 0.0, jnp.where(even, from_a, from_b))
    return before, after


def split(values, lower):
    half = values.shape[0] // 2
    top, bottom = values[:half], values[half:]
    return jnp.where(lower, top, bottom), jnp.where(lower, bottom, top)


def joined(kept, other, lower):
    return jnp.concatenate([jnp.where(lower, kept, other), jnp.where(lower, other, kept)], axis=0)


def tied(*values):
    return lax.optimization_barrier(values)


def shape32(*dims):
    return jax.ShapeDtypeStruct(dims, jnp.float32)


def work(amount):
    return pl.CostEstimate(flops=amount * 10**9, bytes_accessed=2**20, transcendentals=0)


def vmem32(*dims):
    return pltpu.VMEM(dims, jnp.float32)


PARAMS = pltpu.CompilerParams(vmem_limit_bytes=32 * 1024 * 1024)


def on_device(modes, mean_flow, seeds, amplitudes, water_mask):
    count, _, nx, ny = modes.shape
    devices = lax.axis_size("row") * lax.axis_size("col")
    rows_dev = seeds.shape[0]
    row_total = rows_dev * devices
    scale = 1.0 / (2.0 * nx * ny * devices)
    pairs, padded, first, second, share = pair_layout(count)
    tiles = padded // LANES
    fields = count + TILE
    total = 2 * (nx + 4)
    assert ny == LANES and 2 * (nx + 2) <= SECOND and count % (2 * TILE) == 0
    call = functools.partial(pl.pallas_call, compiler_params=PARAMS)
    assert min(lax.axis_size("row"), lax.axis_size("col")) >= 4

    first_row = lax.axis_index(("row", "col")) * rows_dev
    row_ids = (first_row + jnp.arange(rows_dev, dtype=jnp.int32)).astype(jnp.float32)
    strength = (0.5 + row_ids / row_total).reshape(1, rows_dev)
    planes, sums, early, coeffs = call(
        functools.partial(front_kernel, scale),
        out_shape=(
            shape32(total, fields, ny), shape32(tiles * count, LANES), shape32(count // 2, LANES),
            shape32(count, rows_dev),
        ),
        scratch_shapes=[vmem32(padded, rows_dev)],
    )(
        modes.reshape(count * 2 * nx, ny), mean_flow.reshape(2 * nx, ny), water_mask, seeds.T,
        strength, amplitudes.reshape(1, count),
    )

    *grads, own_first, own_last = call(
        plain_gradient_kernel,
        out_shape=(
            shape32(2 * nx, fields, ny), shape32(2 * nx, fields, ny), shape32(fields, ny), shape32(fields, ny),
        ),
    )(planes)

    def tensor_piece(number, grads, *before):
        start, stop = nx * number // 3, nx * (number + 1) // 3
        return call(
            functools.partial(tensor_kernel, scale, start, stop),
            out_shape=shape32(tiles * count, LANES),
            scratch_shapes=[vmem32(padded, 2 * ny)],
        )(planes, *grads, *before)

    near_top, far_top = planes[4:6], planes[6:8]
    far_bottom, near_bottom = planes[total - 8 : total - 6], planes[total - 6 : total - 4]
    row, col = lax.axis_index("row"), lax.axis_index("col")
    even_row, even_col = row % 2 == 0, col % 2 == 0
    lower_a, lower_b = (row + 1) // 2 % 2 == 0, row % 2 == 1
    row_a, row_b = pairs_a("row"), shifted("row", 1)
    col_a, col_b = pairs_a("col"), shifted("col", 1)

    kept, sent = split(sums, lower_a)
    by_way = lax.axis_size("row") == 4
    far_out = jnp.where(even_row, far_top, far_bottom)
    arrived, extra, near_a, far_a, *far_way = with_edges(
        "row", row_a, sent, early[None],
        jnp.where(even_row, near_bottom, near_top), jnp.where(even_row, far_bottom, far_top),
        *([far_out] if by_way else []),
    )
    kept, early, own_first, *grads = tied(kept + arrived, early + extra[0], own_first, *grads)
    near_out = jnp.where(even_row, near_top, near_bottom)
    if by_way:
        outer = (row == 0) | (row == lax.axis_size("row") - 1)
        edges_out = [jnp.where(outer, far_way[0], near_out)]
    else:
        edges_out = [near_out, far_out]
    kept, sent = split(kept, lower_b)
    arrived, extra, near_b, *far_b = with_edges("row", row_b, sent, early[None], *edges_out)
    above, below = neighbours("row", near_a, near_b)
    tensor = tensor_piece(0, grads)
    kept, early, above, below, tensor = tied(kept + arrived, early + extra[0], above, below, tensor)
    extended, col_first, col_last = call(
        extend_kernel,
        out_shape=(shape32(total, fields, ny), shape32(fields, ny), shape32(fields, ny)),
    )(planes, above, below, own_first, own_last)
    first_edge, last_edge = col_first[None], col_last[None]
    arrived, extra, col_from_a = with_edges("col", col_a, kept, early[None], jnp.where(even_col, last_edge, first_edge))
    tensor = tensor_piece(1, grads, tensor)
    kept, early, tensor = tied(kept + arrived, early + extra[0], tensor)
    arrived, extra, col_from_b = with_edges("col", col_b, kept, early[None], jnp.where(even_col, first_edge, last_edge))
    left, right = (edge[0] for edge in neighbours("col", col_from_a, col_from_b))
    tensor = tensor_piece(2, grads, tensor)
    kept, early, left, right, tensor = tied(kept + arrived, early + extra[0], left, right, tensor)

    later = later_steps("row") + later_steps("col")
    for number, (axis, partner) in enumerate(later):
        arrived, extra = with_edges(axis, partner, kept, early[None])
        kept, early = kept + arrived, early + extra[0]
        if number == 0:
            tensor = call(
                functools.partial(edge_tensor_kernel, scale),
                out_shape=shape32(tiles * count, LANES),
                scratch_shapes=[vmem32(6, fields, ny), vmem32(padded, 5 * ny)],
            )(extended, left, right, col_first, col_last, tensor)
            grad_x, grad_y, ring, shape = call(
                gradient_kernel,
                out_shape=(
                    shape32(total - 4, fields, ny), shape32(total - 4, fields, ny), shape32(5, fields, ny),
                    shape32(2 * nx, count, ny),
                ),
            )(extended, left, right, col_first, col_last)
        kept, early, tensor, shape = tied(kept, early, tensor, shape)
    moments = kept

    kept, sent = split(tensor, lower_a)
    arrived, *far_way = with_edges("row", row_a, sent, *([near_b] if by_way else []))
    far_above, far_below = neighbours("row", far_a, (far_way if by_way else far_b)[0])
    both, mean, pair_cov, offset = call(
        functools.partial(offset_kernel, row_total),
        out_shape=(
            shape32(2, count, count), shape32(count, rows_dev), shape32(1, padded), shape32(count, padded),
        ),
    )(early, first, second, share)
    kept, moments, both, far_above = tied(kept + arrived, moments, both, far_above)
    kept, sent = split(kept, lower_b)
    arrived, other = with_edges("row", row_b, sent, moments[None])
    kept = kept + arrived
    cov_inverse, gram_inverse = call(
        inverse_kernel, out_shape=(shape32(count, count), shape32(count, count))
    )(both)
    moments = joined(moments, other[0], lower_b)
    kept, moments, cov_inverse = tied(kept, moments, cov_inverse)
    moments, late_coeffs = tied(moments, coeffs)
    pieces = call(
        pair_kernel,
        out_shape=jax.ShapeDtypeStruct((2 * padded, rows_dev), jnp.bfloat16),
        scratch_shapes=[vmem32(padded, rows_dev)],
    )(late_coeffs, mean)
    sums = joined(moments, swap(moments, "row", row_a), lower_a)
    kept, pieces = tied(kept, pieces)
    col_bits = axis_bits("col")
    steps = later_steps("row") + [
        ("col", [i ^ (1 << bit) for i in range(lax.axis_size("col"))]) for bit in col_bits[:1] + col_bits[:0:-1]
    ]

    def forcing(weights, start, stop):
        return call(
            functools.partial(forcing_kernel, start),
            cost_estimate=work(3),
            out_shape=shape32(2 * (stop - start), count, ny),
            scratch_shapes=[vmem32(padded, 2 * ny)],
        )(weights, extended, grad_x, grad_y)

    weights = None
    moved = []
    for number, (axis, partner) in enumerate(steps):
        total_kept = kept + swap(kept, axis, partner)
        if number == 0:
            kept, sums = tied(total_kept, sums)
            continue
        if weights is None:
            weights = call(
                functools.partial(weight_kernel, row_total),
                cost_estimate=work(1),
                out_shape=jax.ShapeDtypeStruct((2 * count, padded), jnp.bfloat16),
            )(sums, cov_inverse, offset, share)
        if number < 3:
            moved.append(forcing(weights, 1 + nx * (number - 1) // 2, 1 + nx * number // 2))
        kept, weights, moved = tied(total_kept, weights, moved)
    kept = joined(kept, swap(kept, "row", row_b), lower_b)
    base = call(
        closing_kernel,
        out_shape=shape32(2 * nx, count, ny),
        scratch_shapes=[vmem32(4, count, ny), vmem32(4, fields, ny), vmem32(padded, 2 * ny)],
    )(weights, extended, far_above, far_below, grad_y, ring, *moved)
    kept, base = tied(kept, base)
    tensor = joined(kept, swap(kept, "row", row_a), lower_a)

    new_modes, new_coeffs = call(
        finish_kernel,
        out_shape=(shape32(count * 2 * nx, ny), shape32(count, rows_dev)),
        out_specs=(pl.BlockSpec(memory_space=pltpu.HBM),) * 2,
        scratch_shapes=[vmem32(count * 2 * nx, ny), vmem32(count, rows_dev), pltpu.SemaphoreType.DMA((2,))],
    )(tensor, weights, pieces, gram_inverse, coeffs, mean, pair_cov, share, base, shape)
    return (new_modes.reshape(modes.shape), new_coeffs.T)


def solution(mesh):
    return jax.shard_map(
        on_device,
        mesh=mesh,
        in_specs=(
            P(None, None, "row", "col"),
            P(None, "row", "col"),
            P(("row", "col"), None),
            P(),
            P("row", "col"),
        ),
        out_specs=(P(None, None, "row", "col"), P(("row", "col"), None)),
        check_vma=False,
    )
```
